256 devices in a mesh: ia: 8 (over z), ja: 8 (over y, core), ka: 4 (over x).
Axes of the slice: x: 4, y: 4, z: 8, core: 2. Of those that a mesh axis runs over, the one named last changes fastest.
Arguments:
- tensor: bfloat16 [4096, 64, 4096], P('ia', 'ka', 'ja'), may hold values from -6 to 6
- factor_b: float32 [4096, 32], P(('ja', 'ia')), may hold values from -1 to 1, as said below
- factor_c: float32 [64, 32], P('ka'), may hold values from -1 to 1, as said below
Outputs:
- factor_a: float32 [4096, 32], P(('ia', 'ja', 'ka'))
The draws below stay inside these ranges and needn't reach their ends.
Inputs may be any that keep to these rules, and one draw needn't show every extreme that they name: `factor_b`: dense real entries; columns of different scales with a part common to all columns. `factor_c`: dense real entries; columns of different scales with a part common to all columns.
All inputs are finite; a program needn't handle non-finite values.
Results may differ from the reference program's by a relative error of at most 0.0041.
Values sent between devices are 32-bit elements; how exact they have to be, the bound alone decides.
A program may use at most 64 MiB of HBM per device.

```python
import math
import jax
import jax.numpy as jnp
from jax import lax

RANK = 32
I = 4096
J = 4096
K = 64


def draw_factor_b(key, part):
    key = jax.random.fold_in(key, 11)
    first, second, third = jax.random.split(key, 3)
    base = jnp.clip(jax.random.normal(first, (J, RANK), jnp.float32), -3.5, 3.5)
    common = 0.5 * jnp.clip(jax.random.normal(second, (J, 1), jnp.float32), -3.5, 3.5)
    scales = jnp.exp(jax.random.uniform(third, (1, RANK), jnp.float32, math.log(0.4), math.log(2.5)))
    return jnp.clip((base + common) * scales / math.sqrt(J), -1.0, 1.0)


def draw_factor_c(key, part):
    key = jax.random.fold_in(key, 23)
    first, second, third = jax.random.split(key, 3)
    base = jnp.clip(jax.random.normal(first, (K, RANK), jnp.float32), -3.5, 3.5)
    common = 0.5 * jnp.clip(jax.random.normal(second, (K, 1), jnp.float32), -3.5, 3.5)
    scales = jnp.exp(jax.random.uniform(third, (1, RANK), jnp.float32, math.log(0.4), math.log(2.5)))
    return jnp.clip((base + common) * scales / math.sqrt(K), -1.0, 1.0)


def shard_levels(own_key, extent, cuts, smallest, top_value):
    def one(position, blocks):
        heights = jax.random.uniform(jax.random.fold_in(jax.random.fold_in(own_key, 6), position), (blocks,), jnp.float32, smallest / len(cuts), top_value / len(cuts))
        return jnp.repeat(jnp.exp(heights), extent[position] // blocks).reshape((-1,) + (1,) * (len(extent) - position - 1))

    factor_of = one(*cuts[0])
    for cut in cuts[1:]:
        factor_of = factor_of * one(*cut)
    return factor_of


def normal_values(key, extent, deviation, limit, pieces=(), dtype=jnp.bfloat16):
    loudness = shard_levels(key, extent, pieces, -0.22, 0.18) if pieces else 1.0
    entries = jax.random.normal(key, extent, jnp.float32) * deviation * loudness
    return jnp.minimum(jnp.maximum(entries, -limit), limit).astype(dtype)


def setup_inputs(seed: int = 0) -> dict:
    keys = jax.random.split(jax.random.key(seed), 4)
    tensor = normal_values(keys[0], (I, K, J), 1.0, 6.0, ((0, 8), (1, 4), (2, 8)))
    factor_b = draw_factor_b(jax.random.fold_in(keys[3], 71), 0)
    factor_c = draw_factor_c(jax.random.fold_in(keys[3], 71), 0)
    return dict(tensor=tensor, factor_b=factor_b, factor_c=factor_c)


def apply_inverse(matrix, lower_factor):
    return jax.scipy.linalg.solve_triangular(lower_factor, matrix.T, lower=True).T

def reference(tensor, factor_b, factor_c):
    highest = lax.Precision.HIGHEST
    gram_b = jnp.dot(factor_b.T, factor_b, precision=highest)
    gram_c = jnp.dot(factor_c.T, factor_c, precision=highest)
    low_b = jnp.linalg.cholesky(gram_b)
    low_c = jnp.linalg.cholesky(gram_c)
    q_b = apply_inverse(factor_b, low_b).astype(jnp.bfloat16)
    q_c = apply_inverse(factor_c, low_c).astype(jnp.bfloat16)
    flat = jnp.dot(tensor.reshape(I * K, J).astype(jnp.float32), q_b.astype(jnp.float32), preferred_element_type=jnp.float32).reshape(I, K, RANK)
    core = jnp.einsum('iks,kt->its', flat, q_c.astype(jnp.float32), precision=highest).reshape(I, RANK * RANK)
    kron_r = (low_c.T[:, None, :] * low_b.T[None, :, :]).reshape(RANK * RANK, RANK)
    low_zero = jnp.linalg.cholesky(gram_c * gram_b)
    q_zero = apply_inverse(kron_r, low_zero)
    projected = jnp.dot(core, q_zero, precision=highest)
    return jax.scipy.linalg.solve_triangular(low_zero, projected.T, lower=True, trans=1).T
```

```python
import functools

import jax
import jax.numpy as jnp
from jax import lax
from jax.experimental import pallas as pl
from jax.experimental.pallas import tpu as pltpu
from jax.sharding import PartitionSpec as P

MESH = pl.DeviceIdType.MESH
HIGHEST = lax.Precision.HIGHEST
F32 = jnp.float32
BF16 = jnp.bfloat16
LANES = 128


def lane_group(shape, rank):
    return lax.broadcasted_iota(jnp.int32, shape, 1) // rank


def tile_lanes(x):
    return jnp.concatenate([x] * (LANES // x.shape[1]), axis=1)


def pack_rows(x, rank):
    groups = LANES // rank
    m = x.shape[0] // groups
    lane = lane_group((m, LANES), rank)
    packed = x[:m]
    for g in range(1, groups):
        packed = jnp.where(lane == g, x[g * m:(g + 1) * m], packed)
    return packed


def inverse_spd(matrix):
    n = matrix.shape[0]
    row_id = lax.broadcasted_iota(jnp.int32, (n, n), 0)
    lane_id = lax.broadcasted_iota(jnp.int32, (n, n), 1)
    lane_row = lax.broadcasted_iota(jnp.int32, (1, n), 1)
    for k in range(n):
        row = matrix[k:k + 1, :]
        col = matrix[:, k:k + 1]
        inv = 1.0 / matrix[k:k + 1, k:k + 1]
        scaled = jnp.where(lane_row == k, inv, row * inv)
        rest = jnp.where(lane_id == k, 0.0, matrix)
        matrix = jnp.where(row_id == k, scaled, rest - col * scaled)
    return matrix


def kernel(sizes, tensor_ref, fbt_ref, fc_ref, out_ref,
           tbuf, fbt_own, fc_own, fb_send, fb_all, gc_all, gb_all, weights, send, recv,
           load_sem, own_sem, fb_s, fb_r, gc_s, gc_r, gb_s, gb_r, m_s, m_r):
    n_ia, n_ja, n_ka = sizes
    ia, ja, ka = lax.axis_index("ia"), lax.axis_index("ja"), lax.axis_index("ka")
    rank, shard = fbt_own.shape
    block_k = tbuf.shape[1]
    block_j = tbuf.shape[2]
    rows = out_ref.shape[0]
    group_rows = rows * n_ka
    groups = LANES // rank

    def up(index, by, size):
        return lax.rem(index + by, size)

    own_b = pltpu.make_async_copy(fbt_ref, fbt_own, own_sem.at[0])
    own_c = pltpu.make_async_copy(fc_ref, fc_own, own_sem.at[1])
    own_b.start()
    own_c.start()

    def load(step):
        first = pl.multiple_of(up(ja, step + 1, n_ja) * group_rows, group_rows)
        part = pl.ds(first, group_rows)
        return pltpu.make_async_copy(tensor_ref.at[part], tbuf.at[part], load_sem.at[step])

    @pl.loop(0, n_ja)
    def _(step):
        load(step).start()

    barrier = pltpu.get_barrier_semaphore()

    @pl.loop(1, n_ia)
    def _(d):
        pl.semaphore_signal(barrier, inc=1, device_id={"ia": up(ia, d, n_ia)}, device_id_type=MESH)

    @pl.loop(1, n_ja * n_ka)
    def _(d):
        pl.semaphore_signal(barrier, inc=1, device_id={"ja": up(ja, d // n_ka, n_ja), "ka": up(ka, d % n_ka, n_ka)}, device_id_type=MESH)

    own_b.wait()
    own_c.wait()
    half = rank // 2
    own = fbt_own[...]
    packed_b = jnp.concatenate([own[:half], own[half:]], axis=1)
    fb_send[...] = packed_b
    fb_all[ia] = packed_b
    fc_tiled = tile_lanes(fc_own[...])
    gc_all[0] = pack_rows(
        lax.dot_general(fc_own[...], fc_tiled, (((0,), (0,)), ((), ())), precision=HIGHEST, preferred_element_type=F32), rank)
    pl.semaphore_wait(barrier, n_ia - 1 + n_ja * n_ka - 1)

    @pl.loop(1, n_ia)
    def _(d):
        pltpu.make_async_remote_copy(fb_send, fb_all.at[ia], fb_s, fb_r, device_id={"ia": up(ia, d, n_ia)}, device_id_type=MESH).start()

    @pl.loop(1, n_ka)
    def _(d):
        pltpu.make_async_remote_copy(gc_all.at[0], gc_all.at[n_ka - d], gc_s, gc_r, device_id={"ka": up(ka, d, n_ka)}, device_id_type=MESH).start()

    fb_part = fb_all.at[pl.ds(0, n_ia - 1)]
    pltpu.make_async_copy(fb_part, fb_part, fb_r).wait()

    uppers, lowers = [], []
    for s in range(n_ia):
        piece = fb_all[s]
        uppers.append(piece[:, :shard])
        lowers.append(piece[:, shard:])
    fbt = jnp.concatenate([jnp.concatenate(uppers, axis=1), jnp.concatenate(lowers, axis=1)], axis=0)
    high = fbt.astype(BF16)
    rest = fbt - high.astype(F32)
    middle = rest.astype(BF16)
    low = (rest - middle.astype(F32)).astype(BF16)
    stacked = jnp.concatenate([high.astype(F32), middle.astype(F32), low.astype(F32), jnp.zeros_like(fbt)], axis=0)
    weights[...] = stacked.T.astype(BF16)

    gb_all[0] = pack_rows(
        lax.dot_general(fbt, jnp.concatenate([fbt] * groups, axis=0), (((1,), (1,)), ((), ())), precision=HIGHEST, preferred_element_type=F32), rank)

    @pl.loop(1, n_ja)
    def _(d):
        pltpu.make_async_remote_copy(gb_all.at[0], gb_all.at[n_ja - d], gb_s, gb_r, device_id={"ja": up(ja, d, n_ja)}, device_id_type=MESH).start()

    def contract(step):
        load(step).wait()
        first = pl.multiple_of(up(ja, step + 1, n_ja) * group_rows, group_rows)
        x = tbuf[pl.ds(first, group_rows)].reshape(group_rows * block_k, block_j)
        flat = jnp.dot(x, weights[...], preferred_element_type=F32).reshape(group_rows, block_k, LANES)
        part = jnp.sum(flat * fc_tiled[None], axis=1)
        part = part + pltpu.roll(part, 2 * rank, 1)
        part = part + pltpu.roll(part, rank, 1)
        for b in range(n_ka):
            send[step * n_ka + b] = pack_rows(part[b * rows:(b + 1) * rows], rank)

    def push(step, dk):
        to_j, to_k = up(ja, step + 1, n_ja), up(ka, dk, n_ka)
        slot = (n_ja - 1 - step) * n_ka + (n_ka - dk) % n_ka
        pltpu.make_async_remote_copy(
            send.at[step * n_ka + to_k], recv.at[slot], m_s, m_r, device_id={"ja": to_j, "ka": to_k}, device_id_type=MESH).start()

    @pl.loop(0, n_ja - 1)
    def _(step):
        contract(step)
        for dk in range(n_ka):
            push(step, dk)

    contract(n_ja - 1)
    for dk in range(1, n_ka):
        push(n_ja - 1, dk)
    recv[0] = send[(n_ja - 1) * n_ka + ka]

    gc_part = gc_all.at[pl.ds(1, n_ka - 1)]
    gb_part = gb_all.at[pl.ds(1, n_ja - 1)]
    pltpu.make_async_copy(gc_part, gc_part, gc_r).wait()
    pltpu.make_async_copy(gb_part, gb_part, gb_r).wait()
    gram = jnp.sum(gc_all[...], axis=0) * jnp.sum(gb_all[...], axis=0)
    gram = jnp.concatenate([gram[:, g * rank:(g + 1) * rank] for g in range(groups)], axis=0)
    inverse = jnp.concatenate([inverse_spd(gram)] * groups, axis=0)

    m_part = recv.at[pl.ds(1, n_ja * n_ka - 1)]
    pltpu.make_async_copy(m_part, m_part, m_r).wait()
    total = jnp.sum(recv[...], axis=0)
    lane = lane_group(total.shape, rank)
    spread = jnp.concatenate([jnp.where(lane == g, total, 0.0) for g in range(groups)], axis=0)
    out_ref[...] = jnp.dot(spread, inverse, precision=HIGHEST, preferred_element_type=F32)

    pltpu.make_async_copy(fb_part, fb_part, fb_s).wait()
    pltpu.make_async_copy(gc_part, gc_part, gc_s).wait()
    pltpu.make_async_copy(gb_part, gb_part, gb_s).wait()
    pltpu.make_async_copy(m_part, m_part, m_s).wait()


def solution(mesh):
    sizes = (mesh.shape["ia"], mesh.shape["ja"], mesh.shape["ka"])
    n_ia, n_ja, n_ka = sizes

    def per_device(tensor, factor_b, factor_c):
        block_i, block_k, block_j = tensor.shape
        shard, rank = factor_b.shape
        rows = block_i // (n_ja * n_ka)
        groups = LANES // rank
        dma = pltpu.SemaphoreType.DMA
        vmem = pltpu.VMEM
        return pl.pallas_call(
            functools.partial(kernel, sizes),
            out_shape=jax.ShapeDtypeStruct((rows, rank), F32),
            in_specs=[pl.BlockSpec(memory_space=pltpu.HBM)] * 3,
            out_specs=pl.BlockSpec(memory_space=pltpu.VMEM),
            scratch_shapes=[
                vmem((block_i, block_k, block_j), BF16),
                vmem((rank, shard), F32),
                vmem((block_k, rank), F32),
                vmem((rank // 2, 2 * shard), F32),
                vmem((n_ia, rank // 2, 2 * shard), F32),
                vmem((n_ka, rank // groups, LANES), F32),
                vmem((n_ja, rank // groups, LANES), F32),
                vmem((block_j, LANES), BF16),
                vmem((n_ja * n_ka, rows // groups, LANES), F32),
                vmem((n_ja * n_ka, rows // groups, LANES), F32),
                dma((n_ja,)), dma((2,)),
                dma, dma, dma, dma, dma, dma, dma, dma,
            ],
            compiler_params=pltpu.CompilerParams(collective_id=0, has_side_effects=True, vmem_limit_bytes=56 << 20),
        )(tensor, factor_b.T, factor_c)

    return jax.shard_map(
        per_device,
        mesh=mesh,
        in_specs=(P("ia", "ka", "ja"), P(("ja", "ia"), None), P("ka", None)),
        out_specs=P(("ia", "ja", "ka"), None),
        check_vma=False,
    )
```

```python
import functools

import jax
import jax.numpy as jnp
from jax import lax
from jax.experimental import pallas as pl
from jax.experimental.pallas import tpu as pltpu
from jax.sharding import PartitionSpec as P

MESH = pl.DeviceIdType.MESH
HIGHEST = lax.Precision.HIGHEST
F32 = jnp.float32
BF16 = jnp.bfloat16
LANES = 128


def lane_group(shape, rank):
    return lax.broadcasted_iota(jnp.int32, shape, 1) // rank


def tile_lanes(x):
    return jnp.concatenate([x] * (LANES // x.shape[1]), axis=1)


def pack_rows(x, rank):
    groups = LANES // rank
    m = x.shape[0] // groups
    lane = lane_group((m, LANES), rank)
    packed = x[:m]
    for g in range(1, groups):
        packed = jnp.where(lane == g, x[g * m:(g + 1) * m], packed)
    return packed


def inverse_spd(matrix):
    n = matrix.shape[0]
    row_id = lax.broadcasted_iota(jnp.int32, (n, n), 0)
    lane_id = lax.broadcasted_iota(jnp.int32, (n, n), 1)
    lane_row = lax.broadcasted_iota(jnp.int32, (1, n), 1)
    for k in range(n):
        row = matrix[k:k + 1, :]
        col = matrix[:, k:k + 1]
        inv = 1.0 / matrix[k:k + 1, k:k + 1]
        scaled = jnp.where(lane_row == k, inv, row * inv)
        rest = jnp.where(lane_id == k, 0.0, matrix)
        matrix = jnp.where(row_id == k, scaled, rest - col * scaled)
    return matrix


def kernel(sizes, tensor_ref, fbt_ref, fc_ref, out_ref,
           tbuf, fbt_own, fc_own, fb_send, fb_all, gc_all, gb_all, weights, sums, send, recv,
           load_sem, own_sem, line_sem, plane_sem, fb_s, fb_r, gc_s, gc_r, gb_s, gb_r, m_s, m_r):
    n_ia, n_ja, n_ka = sizes
    n_plane = n_ja * n_ka
    ia, ja, ka = lax.axis_index("ia"), lax.axis_index("ja"), lax.axis_index("ka")
    place = ja * n_ka + ka
    half = n_ia // 2
    mine = ia // half
    rank, shard = fbt_own.shape
    block_k = tbuf.shape[1]
    rows = out_ref.shape[0]
    group_rows = rows * n_ka
    groups = LANES // rank
    depth = half * shard

    def up(index, by, size):
        return lax.rem(index + by, size)

    def in_line(z):
        return {"ia": z}

    def in_plane(p):
        return {"ja": p // n_ka, "ka": p % n_ka}

    own_b = pltpu.make_async_copy(fbt_ref, fbt_own, own_sem.at[0])
    own_c = pltpu.make_async_copy(fc_ref, fc_own, own_sem.at[1])
    own_b.start()
    own_c.start()

    barrier = pltpu.get_barrier_semaphore()

    @pl.loop(ia + 1, n_ia)
    def _(z):
        pl.semaphore_signal(barrier, inc=1, device_id=in_line(z), device_id_type=MESH)

    @pl.loop(place + 1, n_plane)
    def _(p):
        pl.semaphore_signal(barrier, inc=1, device_id=in_plane(p), device_id_type=MESH)

    def load(step):
        part = pl.ds(step * group_rows, group_rows)
        return pltpu.make_async_copy(tensor_ref.at[part], tbuf.at[part], load_sem.at[step])

    @pl.loop(0, n_ja)
    def _(step):
        load(step).start()

    own_b.wait()
    own_c.wait()
    packed_rows = rank // 2
    own = fbt_own[...]
    packed_b = jnp.concatenate([own[:packed_rows], own[packed_rows:]], axis=1)
    fb_send[...] = packed_b
    fb_all[ia] = packed_b
    fc_tiled = tile_lanes(fc_own[...])
    gc_all[0] = pack_rows(
        lax.dot_general(fc_own[...], fc_tiled, (((0,), (0,)), ((), ())), precision=HIGHEST, preferred_element_type=F32), rank)

    def push_rows(z):
        pltpu.make_async_remote_copy(
            fb_send, fb_all.at[ia], fb_s, fb_r.at[mine], device_id=in_line(z), device_id_type=MESH).start()

    def answer_rows(z):
        pl.semaphore_wait(line_sem.at[z], 1)
        push_rows(z)

    @pl.when(ia + place > 0)
    def _():
        pl.semaphore_wait(barrier, ia + place)

    pl.semaphore_signal(plane_sem, inc=1)

    @pl.loop(0, ia)
    def _(z):
        push_rows(z)

    @pl.loop(0, ia)
    def _(z):
        pl.semaphore_signal(line_sem.at[ia], inc=1, device_id=in_line(z), device_id_type=MESH)

    @pl.loop(0, place)
    def _(p):
        pl.semaphore_signal(plane_sem, inc=1, device_id=in_plane(p), device_id_type=MESH)

    pl.loop(ia + 1, (mine + 1) * half)(answer_rows)

    def await_rows(which, count):
        part = fb_all.at[pl.ds(0, count)]
        pltpu.make_async_copy(part, part, fb_r.at[which]).wait()

    def prepare(which):
        uppers, lowers = [], []
        for s in range(half):
            piece = fb_all[which * half + s]
            uppers.append(piece[:, :shard])
            lowers.append(piece[:, shard:])
        fbt = jnp.concatenate([jnp.concatenate(uppers, axis=1), jnp.concatenate(lowers, axis=1)], axis=0)
        high = fbt.astype(BF16)
        rest = fbt - high.astype(F32)
        middle = rest.astype(BF16)
        low = (rest - middle.astype(F32)).astype(BF16)
        stacked = jnp.concatenate([high.astype(F32), middle.astype(F32), low.astype(F32), jnp.zeros_like(fbt)], axis=0)
        weights[...] = stacked.T.astype(BF16)
        gram = lax.dot_general(fbt, jnp.concatenate([fbt] * groups, axis=0), (((1,), (1,)), ((), ())),
                               precision=HIGHEST, preferred_element_type=F32)
        return pack_rows(gram, rank)

    def contract(step, which):
        columns = pl.ds(pl.multiple_of(which * depth, depth), depth)
        x = tbuf[pl.ds(step * group_rows, group_rows), :, columns].reshape(group_rows * block_k, depth)
        flat = jnp.dot(x, weights[...], preferred_element_type=F32).reshape(group_rows, block_k, LANES)
        return jnp.sum(flat * fc_tiled[None], axis=1)

    pl.loop(half + mine * half, n_ia)(answer_rows)
    await_rows(mine, half - 1)
    gb_all[0] = prepare(mine)

    @pl.loop(0, n_ja)
    def _(step):
        load(step).wait()

    @pl.loop(0, n_ja, unroll=n_ja)
    def _(step):
        sums[step] = contract(step, mine)

    pl.semaphore_wait(plane_sem, n_plane - place)

    @pl.loop(1, n_ka)
    def _(d):
        pltpu.make_async_remote_copy(gc_all.at[0], gc_all.at[n_ka - d], gc_s, gc_r, device_id={"ka": up(ka, d, n_ka)}, device_id_type=MESH).start()

    await_rows(1 - mine, half)
    gb_all[0] = gb_all[0] + prepare(1 - mine)

    @pl.loop(1, n_ja)
    def _(d):
        pltpu.make_async_remote_copy(gb_all.at[0], gb_all.at[n_ja - d], gb_s, gb_r, device_id={"ja": up(ja, d, n_ja)}, device_id_type=MESH).start()

    def finish(step):
        part = sums[step] + contract(step, 1 - mine)
        part = part + pltpu.roll(part, 2 * rank, 1)
        part = part + pltpu.roll(part, rank, 1)
        for b in range(n_ka):
            send[step * n_ka + b] = pack_rows(part[b * rows:(b + 1) * rows], rank)

    pl.loop(0, n_ja, unroll=n_ja)(finish)
    for dj in sorted(range(n_ja), key=lambda d: -min(d, n_ja - d)):
        for dk in sorted(range(n_ka), key=lambda d: -min(d, n_ka - d)):
            if dj or dk:
                to_j, to_k = up(ja, dj, n_ja), up(ka, dk, n_ka)
                slot = (n_ja - dj) % n_ja * n_ka + (n_ka - dk) % n_ka
                pltpu.make_async_remote_copy(
                    send.at[to_j * n_ka + to_k], recv.at[slot], m_s, m_r,
                    device_id={"ja": to_j, "ka": to_k}, device_id_type=MESH).start()
    recv[0] = send[place]

    gc_part = gc_all.at[pl.ds(1, n_ka - 1)]
    gb_part = gb_all.at[pl.ds(1, n_ja - 1)]
    pltpu.make_async_copy(gc_part, gc_part, gc_r).wait()
    pltpu.make_async_copy(gb_part, gb_part, gb_r).wait()
    gram = jnp.sum(gc_all[...], axis=0) * jnp.sum(gb_all[...], axis=0)
    gram = jnp.concatenate([gram[:, g * rank:(g + 1) * rank] for g in range(groups)], axis=0)
    inverse = jnp.concatenate([inverse_spd(gram)] * groups, axis=0)

    fb_part = fb_all.at[pl.ds(0, n_ia - 1)]
    pltpu.make_async_copy(fb_part, fb_part, fb_s).wait()
    pltpu.make_async_copy(gc_part, gc_part, gc_s).wait()
    pltpu.make_async_copy(gb_part, gb_part, gb_s).wait()
    m_part = recv.at[pl.ds(1, n_plane - 1)]
    pltpu.make_async_copy(m_part, m_part, m_s).wait()
    pltpu.make_async_copy(m_part, m_part, m_r).wait()
    total = jnp.sum(recv[...], axis=0)
    lane = lane_group(total.shape, rank)
    spread = jnp.concatenate([jnp.where(lane == g, total, 0.0) for g in range(groups)], axis=0)
    out_ref[...] = jnp.dot(spread, inverse, precision=HIGHEST, preferred_element_type=F32)


def solution(mesh):
    sizes = (mesh.shape["ia"], mesh.shape["ja"], mesh.shape["ka"])
    n_ia, n_ja, n_ka = sizes

    def per_device(tensor, factor_b, factor_c):
        block_i, block_k, block_j = tensor.shape
        shard, rank = factor_b.shape
        rows = block_i // (n_ja * n_ka)
        groups = LANES // rank
        dma = pltpu.SemaphoreType.DMA
        vmem = pltpu.VMEM
        return pl.pallas_call(
            functools.partial(kernel, sizes),
            out_shape=pltpu.VMEM((rows, rank), F32),
            in_specs=[pl.BlockSpec(memory_space=pltpu.HBM)] * 3,
            out_specs=pl.BlockSpec(memory_space=pltpu.VMEM),
            scratch_shapes=[
                vmem((block_i, block_k, block_j), BF16),
                vmem((rank, shard), F32),
                vmem((block_k, rank), F32),
                vmem((rank // 2, 2 * shard), F32),
                vmem((n_ia, rank // 2, 2 * shard), F32),
                vmem((n_ka, rank // groups, LANES), F32),
                vmem((n_ja, rank // groups, LANES), F32),
                vmem((block_j // 2, LANES), BF16),
                vmem((n_ja, rows * n_ka, LANES), F32),
                vmem((n_ja * n_ka, rows // groups, LANES), F32),
                vmem((n_ja * n_ka, rows // groups, LANES), F32),
                dma((n_ja,)), dma((2,)),
                pltpu.SemaphoreType.REGULAR((n_ia,)), pltpu.SemaphoreType.REGULAR,
                dma, dma((2,)), dma, dma, dma, dma, dma, dma,
            ],
            compiler_params=pltpu.CompilerParams(collective_id=0, has_side_effects=True, vmem_limit_bytes=56 << 20),
        )(tensor, factor_b.T, factor_c)

    return jax.shard_map(
        per_device,
        mesh=mesh,
        in_specs=(P("ia", "ka", "ja"), P(("ja", "ia"), None), P("ka", None)),
        out_specs=P(("ia", "ja", "ka"), None),
        check_vma=False,
    )
```

```python
import functools

import jax
import jax.numpy as jnp
from jax import lax
from jax.experimental import pallas as pl
from jax.experimental.pallas import tpu as pltpu
from jax.sharding import PartitionSpec as P

MESH = pl.DeviceIdType.MESH
HIGHEST = lax.Precision.HIGHEST
F32 = jnp.float32
BF16 = jnp.bfloat16
LANES = 128


def lane_group(shape, rank):
    return lax.broadcasted_iota(jnp.int32, shape, 1) // rank


def tile_lanes(x):
    return jnp.concatenate([x] * (LANES // x.shape[1]), axis=1)


def pack_rows(x, rank):
    groups = LANES // rank
    m = x.shape[0] // groups
    lane = lane_group((m, LANES), rank)
    packed = x[:m]
    for g in range(1, groups):
        packed = jnp.where(lane == g, x[g * m:(g + 1) * m], packed)
    return packed


def inverse_spd(matrix, block=8):
    n = matrix.shape[0]
    row_id = lax.broadcasted_iota(jnp.int32, (n, n), 0)
    lane_id = lax.broadcasted_iota(jnp.int32, (n, n), 1)
    lane_row = lax.broadcasted_iota(jnp.int32, (1, n), 1)
    for start in range(0, n, block):
        spread = {j: jnp.broadcast_to(matrix[:, j:j + 1], (n, n)) for j in range(start, start + block)}
        for k in range(start, start + block):
            col = spread[k]
            inv = 1.0 / col[k:k + 1, :]
            scaled = jnp.where(lane_row == k, inv, matrix[k:k + 1, :] * inv)
            rest = jnp.where(lane_id == k, 0.0, matrix)
            matrix = jnp.where(row_id == k, scaled, rest - col * scaled)
            for j in range(k + 1, start + block):
                pivot_row = spread[j][k:k + 1, :] * inv
                spread[j] = jnp.where(row_id == k, pivot_row, spread[j] - col * pivot_row)
    return matrix


def kernel(sizes, tensor_ref, fbt_ref, fc_ref, out_ref,
           tbuf, fbt_own, fc_own, fb_send, fb_all, gc_all, gb_all, weights, sums, send, recv,
           load_sem, own_sem, line_sem, plane_sem, fb_s, fb_r, gc_s, gc_r, gb_s, gb_r, m_s, m_r):
    n_ia, n_ja, n_ka = sizes
    n_plane = n_ja * n_ka
    ia, ja, ka = lax.axis_index("ia"), lax.axis_index("ja"), lax.axis_index("ka")
    place = ja * n_ka + ka
    half = n_ia // 2
    mine = ia // half
    rank, shard = fbt_own.shape
    block_k = tbuf.shape[1]
    rows = out_ref.shape[0]
    group_rows = rows * n_ka
    groups = LANES // rank
    depth = half * shard

    def up(index, by, size):
        return lax.rem(index + by, size)

    def in_line(z):
        return {"ia": z}

    def in_plane(p):
        return {"ja": p // n_ka, "ka": p % n_ka}

    own_b = pltpu.make_async_copy(fbt_ref, fbt_own, own_sem.at[0])
    own_c = pltpu.make_async_copy(fc_ref, fc_own, own_sem.at[1])
    own_b.start()
    own_c.start()

    barrier = pltpu.get_barrier_semaphore()

    @pl.loop(ia + 1, n_ia)
    def _(z):
        pl.semaphore_signal(barrier, inc=1, device_id=in_line(z), device_id_type=MESH)

    @pl.loop(place + 1, n_plane)
    def _(p):
        pl.semaphore_signal(barrier, inc=1, device_id=in_plane(p), device_id_type=MESH)

    def load(step):
        part = pl.ds(pl.multiple_of(step * group_rows, group_rows), group_rows)
        return pltpu.make_async_copy(tensor_ref.at[part], tbuf.at[part], load_sem.at[step])

    @pl.loop(0, n_ja)
    def _(step):
        load(step).start()

    own_b.wait()
    packed_rows = rank // 2
    own = fbt_own[...]
    packed_b = jnp.concatenate([own[:packed_rows], own[packed_rows:]], axis=1)
    fb_send[...] = packed_b
    fb_all[ia] = packed_b

    def push_rows(z):
        pltpu.make_async_remote_copy(
            fb_send, fb_all.at[ia], fb_s, fb_r.at[mine], device_id=in_line(z), device_id_type=MESH).start()

    def answer_rows(z):
        pl.semaphore_wait(line_sem.at[z], 1)
        push_rows(z)

    @pl.when(ia + place > 0)
    def _():
        pl.semaphore_wait(barrier, ia + place)

    pl.semaphore_signal(plane_sem, inc=1)

    @pl.loop(0, ia)
    def _(z):
        push_rows(z)

    @pl.loop(0, ia)
    def _(z):
        pl.semaphore_signal(line_sem.at[ia], inc=1, device_id=in_line(z), device_id_type=MESH)

    @pl.loop(0, place)
    def _(p):
        pl.semaphore_signal(plane_sem, inc=1, device_id=in_plane(p), device_id_type=MESH)

    pl.loop(ia + 1, (mine + 1) * half)(answer_rows)

    def await_rows(which, count):
        part = fb_all.at[pl.ds(0, count)]
        pltpu.make_async_copy(part, part, fb_r.at[which]).wait()

    def prepare(which):
        uppers, lowers = [], []
        for s in range(half):
            piece = fb_all[which * half + s]
            uppers.append(piece[:, :shard])
            lowers.append(piece[:, shard:])
        fbt = jnp.concatenate([jnp.concatenate(uppers, axis=1), jnp.concatenate(lowers, axis=1)], axis=0)
        high = fbt.astype(BF16)
        rest = fbt - high.astype(F32)
        middle = rest.astype(BF16)
        low = (rest - middle.astype(F32)).astype(BF16)
        stacked = jnp.concatenate([high.astype(F32), middle.astype(F32), low.astype(F32), jnp.zeros_like(fbt)], axis=0)
        weights[...] = stacked.T.astype(BF16)
        gram = lax.dot_general(fbt, jnp.concatenate([fbt] * groups, axis=0), (((1,), (1,)), ((), ())),
                               precision=HIGHEST, preferred_element_type=F32)
        return pack_rows(gram, rank)

    def contract(step, which):
        columns = pl.ds(pl.multiple_of(which * depth, depth), depth)
        x = tbuf[pl.ds(pl.multiple_of(step * group_rows, group_rows), group_rows), :, columns].reshape(group_rows * block_k, depth)
        flat = jnp.dot(x, weights[...], preferred_element_type=F32).reshape(group_rows, block_k, LANES)
        return jnp.sum(flat * fc_tiled[None], axis=1)

    own_c.wait()
    fc_tiled = tile_lanes(fc_own[...])
    gc_all[0] = pack_rows(
        lax.dot_general(fc_own[...], fc_tiled, (((0,), (0,)), ((), ())), precision=HIGHEST, preferred_element_type=F32), rank)
    pl.loop(half + mine * half, n_ia)(answer_rows)
    await_rows(mine, half - 1)
    gb_all[0] = prepare(mine)

    @pl.loop(0, n_ja)
    def _(step):
        load(step).wait()

    @pl.loop(0, n_ja, unroll=n_ja)
    def _(step):
        sums[step] = contract(step, mine)

    pl.semaphore_wait(plane_sem, n_plane - place)

    @pl.loop(1, n_ka)
    def _(d):
        pltpu.make_async_remote_copy(gc_all.at[0], gc_all.at[n_ka - d], gc_s, gc_r, device_id={"ka": up(ka, d, n_ka)}, device_id_type=MESH).start()

    await_rows(1 - mine, half)
    gb_all[0] = gb_all[0] + prepare(1 - mine)

    @pl.loop(1, n_ja)
    def _(d):
        pltpu.make_async_remote_copy(gb_all.at[0], gb_all.at[n_ja - d], gb_s, gb_r, device_id={"ja": up(ja, d, n_ja)}, device_id_type=MESH).start()

    def finish(dj):
        step = up(ja, dj, n_ja)
        part = sums[step] + contract(step, 1 - mine)
        part = part + pltpu.roll(part, 2 * rank, 1)
        part = part + pltpu.roll(part, rank, 1)
        for b in range(n_ka):
            send[dj * n_ka + b] = pack_rows(part[b * rows:(b + 1) * rows], rank)

    def push(dj, dk):
        to_j, to_k = up(ja, dj, n_ja), up(ka, dk, n_ka)
        slot = (n_ja - dj) % n_ja * n_ka + (n_ka - dk) % n_ka
        pltpu.make_async_remote_copy(
            send.at[dj * n_ka + to_k], recv.at[slot], m_s, m_r, device_id={"ja": to_j, "ka": to_k}, device_id_type=MESH).start()

    order = sorted(range(n_ja), key=lambda d: -min(d, n_ja - d))
    batch = n_ja // 4
    for first in range(0, n_ja, batch):
        for dj in order[first:first + batch]:
            finish(dj)
        for dk in sorted(range(n_ka), key=lambda d: -min(d, n_ka - d)):
            for dj in order[first:first + batch]:
                if dj or dk:
                    push(dj, dk)
    recv[0] = send[ka]

    gc_part = gc_all.at[pl.ds(1, n_ka - 1)]
    gb_part = gb_all.at[pl.ds(1, n_ja - 1)]
    pltpu.make_async_copy(gc_part, gc_part, gc_r).wait()
    pltpu.make_async_copy(gb_part, gb_part, gb_r).wait()
    gram = jnp.sum(gc_all[...], axis=0) * jnp.sum(gb_all[...], axis=0)
    gram = jnp.concatenate([gram[:, g * rank:(g + 1) * rank] for g in range(groups)], axis=0)
    inverse = jnp.concatenate([inverse_spd(gram)] * groups, axis=0)

    fb_part = fb_all.at[pl.ds(0, n_ia - 1)]
    pltpu.make_async_copy(fb_part, fb_part, fb_s).wait()
    pltpu.make_async_copy(gc_part, gc_part, gc_s).wait()
    pltpu.make_async_copy(gb_part, gb_part, gb_s).wait()
    m_part = recv.at[pl.ds(1, n_plane - 1)]
    pltpu.make_async_copy(m_part, m_part, m_s).wait()
    pltpu.make_async_copy(m_part, m_part, m_r).wait()
    total = jnp.sum(recv[...], axis=0)
    lane = lane_group(total.shape, rank)
    spread = jnp.concatenate([jnp.where(lane == g, total, 0.0) for g in range(groups)], axis=0)
    out_ref[...] = jnp.dot(spread, inverse, precision=HIGHEST, preferred_element_type=F32)


def solution(mesh):
    sizes = (mesh.shape["ia"], mesh.shape["ja"], mesh.shape["ka"])
    n_ia, n_ja, n_ka = sizes

    def per_device(tensor, factor_b, factor_c):
        block_i, block_k, block_j = tensor.shape
        shard, rank = factor_b.shape
        rows = block_i // (n_ja * n_ka)
        groups = LANES // rank
        dma = pltpu.SemaphoreType.DMA
        vmem = pltpu.VMEM
        return pl.pallas_call(
            functools.partial(kernel, sizes),
            out_shape=pltpu.VMEM((rows, rank), F32),
            in_specs=[pl.BlockSpec(memory_space=pltpu.HBM)] * 3,
            out_specs=pl.BlockSpec(memory_space=pltpu.VMEM),
            scratch_shapes=[
                vmem((block_i, block_k, block_j), BF16),
                vmem((rank, shard), F32),
                vmem((block_k, rank), F32),
                vmem((rank // 2, 2 * shard), F32),
                vmem((n_ia, rank // 2, 2 * shard), F32),
                vmem((n_ka, rank // groups, LANES), F32),
                vmem((n_ja, rank // groups, LANES), F32),
                vmem((block_j // 2, LANES), BF16),
                vmem((n_ja, rows * n_ka, LANES), F32),
                vmem((n_ja * n_ka, rows // groups, LANES), F32),
                vmem((n_ja * n_ka, rows // groups, LANES), F32),
                dma((n_ja,)), dma((2,)),
                pltpu.SemaphoreType.REGULAR((n_ia,)), pltpu.SemaphoreType.REGULAR,
                dma, dma((2,)), dma, dma, dma, dma, dma, dma,
            ],
            compiler_params=pltpu.CompilerParams(collective_id=0, has_side_effects=True, vmem_limit_bytes=56 << 20),
        )(tensor, factor_b.T, factor_c)

    return jax.shard_map(
        per_device,
        mesh=mesh,
        in_specs=(P("ia", "ka", "ja"), P(("ja", "ia"), None), P("ka", None)),
        out_specs=P(("ia", "ja", "ka"), None),
        check_vma=False,
    )
```

```python
import functools

import jax
import jax.numpy as jnp
from jax import lax
from jax.experimental import pallas as pl
from jax.experimental.pallas import tpu as pltpu
from jax.sharding import PartitionSpec as P

MESH = pl.DeviceIdType.MESH
HIGHEST = lax.Precision.HIGHEST
F32 = jnp.float32
BF16 = jnp.bfloat16
LANES = 128


def lane_group(shape, rank):
    return lax.broadcasted_iota(jnp.int32, shape, 1) // rank


def tile_lanes(x):
    return jnp.concatenate([x] * (LANES // x.shape[1]), axis=1)


def pack_rows(x, rank):
    groups = LANES // rank
    m = x.shape[0] // groups
    lane = lane_group((m, LANES), rank)
    packed = x[:m]
    for g in range(1, groups):
        packed = jnp.where(lane == g, x[g * m:(g + 1) * m], packed)
    return packed


def inverse_spd(matrix, block=8):
    n = matrix.shape[0]
    row_id = lax.broadcasted_iota(jnp.int32, (n, n), 0)
    lane_id = lax.broadcasted_iota(jnp.int32, (n, n), 1)
    lane_row = lax.broadcasted_iota(jnp.int32, (1, n), 1)
    for start in range(0, n, block):
        spread = {j: jnp.broadcast_to(matrix[:, j:j + 1], (n, n)) for j in range(start, start + block)}
        for k in range(start, start + block):
            col = spread[k]
            inv = 1.0 / col[k:k + 1, :]
            scaled = jnp.where(lane_row == k, inv, matrix[k:k + 1, :] * inv)
            rest = jnp.where(lane_id == k, 0.0, matrix)
            matrix = jnp.where(row_id == k, scaled, rest - col * scaled)
            for j in range(k + 1, start + block):
                pivot_row = spread[j][k:k + 1, :] * inv
                spread[j] = jnp.where(row_id == k, pivot_row, spread[j] - col * pivot_row)
    return matrix


def kernel(sizes, tensor_ref, fbt_ref, fc_ref, out_ref,
           tbuf, fbt_own, fc_own, fb_send, fb_all, gc_all, gb_all, weights, sums, send, recv,
           load_sem, own_sem, line_sem, plane_sem, near_sem, far_sem, fb_s, fb_r, gc_s, gc_r, gb_s, gb_r, m_s, m_r):
    n_ia, n_ja, n_ka = sizes
    n_plane = n_ja * n_ka
    ia, ja, ka = lax.axis_index("ia"), lax.axis_index("ja"), lax.axis_index("ka")
    place = ja * n_ka + ka
    half = n_ia // 2
    mine = ia // half
    rank, shard = fbt_own.shape
    block_k = tbuf.shape[1]
    rows = out_ref.shape[0]
    group_rows = rows * n_ka
    groups = LANES // rank
    depth = half * shard

    def up(index, by, size):
        return lax.rem(index + by, size)

    def in_line(z):
        return {"ia": z}

    def in_plane(p):
        return {"ja": p // n_ka, "ka": p % n_ka}

    own_b = pltpu.make_async_copy(fbt_ref, fbt_own, own_sem.at[0])
    own_c = pltpu.make_async_copy(fc_ref, fc_own, own_sem.at[1])
    own_b.start()
    own_c.start()

    barrier = pltpu.get_barrier_semaphore()

    @pl.loop(ia + 1, n_ia)
    def _(z):
        pl.semaphore_signal(barrier, inc=1, device_id=in_line(z), device_id_type=MESH)

    @pl.when(ia == 0)
    def _():
        @pl.loop(place + 1, n_plane)
        def _(p):
            pl.semaphore_signal(barrier, inc=1, device_id=in_plane(p), device_id_type=MESH)

    def load(step):
        part = pl.ds(pl.multiple_of(step * group_rows, group_rows), group_rows)
        return pltpu.make_async_copy(tensor_ref.at[part], tbuf.at[part], load_sem.at[step])

    @pl.loop(0, n_ja)
    def _(step):
        load(step).start()

    own_b.wait()
    packed_rows = rank // 2
    own = fbt_own[...]
    packed_b = jnp.concatenate([own[:packed_rows], own[packed_rows:]], axis=1)
    fb_send[...] = packed_b
    fb_all[ia] = packed_b

    def push_rows(z):
        pltpu.make_async_remote_copy(
            fb_send, fb_all.at[ia], fb_s, fb_r.at[mine], device_id=in_line(z), device_id_type=MESH).start()

    def answer_rows(z):
        pl.semaphore_wait(line_sem.at[z], 1)
        push_rows(z)

    @pl.when(ia > 0)
    def _():
        pl.semaphore_wait(barrier, ia)

    @pl.when((ia == 0) & (place > 0))
    def _():
        pl.semaphore_wait(barrier, place)

    @pl.loop(0, ia)
    def _(z):
        push_rows(z)

    @pl.loop(0, ia)
    def _(z):
        pl.semaphore_signal(line_sem.at[ia], inc=1, device_id=in_line(z), device_id_type=MESH)

    @pl.when(ia == 0)
    def _():
        pl.semaphore_signal(plane_sem, inc=1)

        @pl.loop(0, place)
        def _(p):
            pl.semaphore_signal(plane_sem, inc=1, device_id=in_plane(p), device_id_type=MESH)

    pl.loop(ia + 1, (mine + 1) * half)(answer_rows)

    def await_rows(which, count):
        part = fb_all.at[pl.ds(0, count)]
        pltpu.make_async_copy(part, part, fb_r.at[which]).wait()

    def prepare(which):
        uppers, lowers = [], []
        for s in range(half):
            piece = fb_all[which * half + s]
            uppers.append(piece[:, :shard])
            lowers.append(piece[:, shard:])
        fbt = jnp.concatenate([jnp.concatenate(uppers, axis=1), jnp.concatenate(lowers, axis=1)], axis=0)
        high = fbt.astype(BF16)
        rest = fbt - high.astype(F32)
        middle = rest.astype(BF16)
        low = (rest - middle.astype(F32)).astype(BF16)
        stacked = jnp.concatenate([high.astype(F32), middle.astype(F32), low.astype(F32), jnp.zeros_like(fbt)], axis=0)
        weights[...] = stacked.T.astype(BF16)
        gram = lax.dot_general(fbt, jnp.concatenate([fbt] * groups, axis=0), (((1,), (1,)), ((), ())),
                               precision=HIGHEST, preferred_element_type=F32)
        return pack_rows(gram, rank)

    def contract(step, which):
        columns = pl.ds(pl.multiple_of(which * depth, depth), depth)
        x = tbuf[pl.ds(pl.multiple_of(step * group_rows, group_rows), group_rows), :, columns].reshape(group_rows * block_k, depth)
        flat = jnp.dot(x, weights[...], preferred_element_type=F32).reshape(group_rows, block_k, LANES)
        return jnp.sum(flat * fc_tiled[None], axis=1)

    own_c.wait()
    fc_tiled = tile_lanes(fc_own[...])
    gc_all[0] = pack_rows(
        lax.dot_general(fc_own[...], fc_tiled, (((0,), (0,)), ((), ())), precision=HIGHEST, preferred_element_type=F32), rank)
    @pl.when(ia == 0)
    def _():
        pl.semaphore_wait(plane_sem, n_plane - place)

        @pl.loop(1, n_plane)
        def _(d):
            pl.semaphore_signal(near_sem, inc=1, device_id=in_plane(lax.rem(place + d, n_plane)), device_id_type=MESH)

    answer_first = ia == half - 1
    answer_later = ia < half - 1

    def answer_far():
        pl.loop(half, n_ia)(answer_rows)

    pl.when(answer_first)(answer_far)
    await_rows(mine, half - 1)
    gb_all[0] = prepare(mine)

    @pl.loop(0, n_ja)
    def _(step):
        load(step).wait()

    @pl.loop(0, n_ja, unroll=n_ja)
    def _(step):
        sums[step] = contract(step, mine)

    pl.when(answer_later)(answer_far)

    def tell(first, end):
        @pl.loop(first, end)
        def _(z):
            pl.semaphore_signal(plane_sem, inc=1, device_id=in_line(z), device_id_type=MESH)

    @pl.when(ia == 0)
    def _():
        @pl.loop(1, n_ka)
        def _(d):
            pl.semaphore_signal(far_sem.at[0], inc=1, device_id={"ka": up(ka, d, n_ka)}, device_id_type=MESH)

        pl.semaphore_wait(near_sem, n_plane - 1)
        tell(1, half)

    await_rows(1 - mine, half)

    @pl.when(ia == 0)
    def _():
        pl.semaphore_wait(far_sem.at[0], n_ka - 1)

        @pl.loop(1, n_ja)
        def _(d):
            pl.semaphore_signal(far_sem.at[1], inc=1, device_id={"ja": up(ja, d, n_ja)}, device_id_type=MESH)

    gb_all[0] = gb_all[0] + prepare(1 - mine)

    @pl.when(ia > 0)
    def _():
        pl.semaphore_wait(plane_sem, 1)

    @pl.loop(1, n_ka)
    def _(d):
        pltpu.make_async_remote_copy(gc_all.at[0], gc_all.at[n_ka - d], gc_s, gc_r, device_id={"ka": up(ka, d, n_ka)}, device_id_type=MESH).start()

    @pl.loop(1, n_ja)
    def _(d):
        pltpu.make_async_remote_copy(gb_all.at[0], gb_all.at[n_ja - d], gb_s, gb_r, device_id={"ja": up(ja, d, n_ja)}, device_id_type=MESH).start()

    def finish(dj):
        step = up(ja, dj, n_ja)
        part = sums[step] + contract(step, 1 - mine)
        part = part + pltpu.roll(part, 2 * rank, 1)
        part = part + pltpu.roll(part, rank, 1)
        for b in range(n_ka):
            send[dj * n_ka + b] = pack_rows(part[b * rows:(b + 1) * rows], rank)

    def push(dj, dk):
        to_j, to_k = up(ja, dj, n_ja), up(ka, dk, n_ka)
        slot = (n_ja - dj) % n_ja * n_ka + (n_ka - dk) % n_ka
        pltpu.make_async_remote_copy(
            send.at[dj * n_ka + to_k], recv.at[slot], m_s, m_r, device_id={"ja": to_j, "ka": to_k}, device_id_type=MESH).start()

    order = sorted(range(n_ja), key=lambda d: -min(d, n_ja - d))
    batch = max(1, n_ja // 2)
    for first in range(0, n_ja, batch):
        for dj in order[first:first + batch]:
            finish(dj)
        for dk in sorted(range(n_ka), key=lambda d: -min(d, n_ka - d)):
            for dj in order[first:first + batch]:
                if dj or dk:
                    push(dj, dk)
    recv[0] = send[ka]

    @pl.when(ia == 0)
    def _():
        pl.semaphore_wait(far_sem.at[1], n_ja - 1)
        tell(half, n_ia)


    gc_part = gc_all.at[pl.ds(1, n_ka - 1)]
    gb_part = gb_all.at[pl.ds(1, n_ja - 1)]
    pltpu.make_async_copy(gc_part, gc_part, gc_r).wait()
    pltpu.make_async_copy(gb_part, gb_part, gb_r).wait()
    gram = jnp.sum(gc_all[...], axis=0) * jnp.sum(gb_all[...], axis=0)
    gram = jnp.concatenate([gram[:, g * rank:(g + 1) * rank] for g in range(groups)], axis=0)
    inverse = jnp.concatenate([inverse_spd(gram)] * groups, axis=0)

    fb_part = fb_all.at[pl.ds(0, n_ia - 1)]
    pltpu.make_async_copy(fb_part, fb_part, fb_s).wait()
    pltpu.make_async_copy(gc_part, gc_part, gc_s).wait()
    pltpu.make_async_copy(gb_part, gb_part, gb_s).wait()
    m_part = recv.at[pl.ds(1, n_plane - 1)]
    pltpu.make_async_copy(m_part, m_part, m_s).wait()
    pltpu.make_async_copy(m_part, m_part, m_r).wait()
    total = jnp.sum(recv[...], axis=0)
    lane = lane_group(total.shape, rank)
    spread = jnp.concatenate([jnp.where(lane == g, total, 0.0) for g in range(groups)], axis=0)
    out_ref[...] = jnp.dot(spread, inverse, precision=HIGHEST, preferred_element_type=F32)


def solution(mesh):
    sizes = (mesh.shape["ia"], mesh.shape["ja"], mesh.shape["ka"])
    n_ia, n_ja, n_ka = sizes

    def per_device(tensor, factor_b, factor_c):
        block_i, block_k, block_j = tensor.shape
        shard, rank = factor_b.shape
        rows = block_i // (n_ja * n_ka)
        groups = LANES // rank
        dma = pltpu.SemaphoreType.DMA
        vmem = pltpu.VMEM
        return pl.pallas_call(
            functools.partial(kernel, sizes),
            out_shape=pltpu.VMEM((rows, rank), F32),
            in_specs=[pl.BlockSpec(memory_space=pltpu.HBM)] * 3,
            out_specs=pl.BlockSpec(memory_space=pltpu.VMEM),
            scratch_shapes=[
                vmem((block_i, block_k, block_j), BF16),
                vmem((rank, shard), F32),
                vmem((block_k, rank), F32),
                vmem((rank // 2, 2 * shard), F32),
                vmem((n_ia, rank // 2, 2 * shard), F32),
                vmem((n_ka, rank // groups, LANES), F32),
                vmem((n_ja, rank // groups, LANES), F32),
                vmem((block_j // 2, LANES), BF16),
                vmem((n_ja, rows * n_ka, LANES), F32),
                vmem((n_ja * n_ka, rows // groups, LANES), F32),
                vmem((n_ja * n_ka, rows // groups, LANES), F32),
                dma((n_ja,)), dma((2,)),
                pltpu.SemaphoreType.REGULAR((n_ia,)), pltpu.SemaphoreType.REGULAR, pltpu.SemaphoreType.REGULAR, pltpu.SemaphoreType.REGULAR((2,)),
                dma, dma((2,)), dma, dma, dma, dma, dma, dma,
            ],
            compiler_params=pltpu.CompilerParams(collective_id=0, has_side_effects=True, vmem_limit_bytes=56 << 20),
        )(tensor, factor_b.T, factor_c)

    return jax.shard_map(
        per_device,
        mesh=mesh,
        in_specs=(P("ia", "ka", "ja"), P(("ja", "ia"), None), P("ka", None)),
        out_specs=P(("ia", "ja", "ka"), None),
        check_vma=False,
    )
```

```python
import functools

import jax
import jax.numpy as jnp
from jax import lax
from jax.experimental import pallas as pl
from jax.experimental.pallas import tpu as pltpu
from jax.sharding import PartitionSpec as P

MESH = pl.DeviceIdType.MESH
HIGHEST = lax.Precision.HIGHEST
F32 = jnp.float32
BF16 = jnp.bfloat16
LANES = 128


def lane_group(shape, rank):
    return lax.broadcasted_iota(jnp.int32, shape, 1) // rank


def tile_lanes(x):
    return jnp.concatenate([x] * (LANES // x.shape[1]), axis=1)


def pack_rows(x, rank):
    groups = LANES // rank
    m = x.shape[0] // groups
    lane = lane_group((m, LANES), rank)
    packed = x[:m]
    for g in range(1, groups):
        packed = jnp.where(lane == g, x[g * m:(g + 1) * m], packed)
    return packed


def inverse_spd(matrix, block=8):
    n = matrix.shape[0]
    row_id = lax.broadcasted_iota(jnp.int32, (n, n), 0)
    lane_id = lax.broadcasted_iota(jnp.int32, (n, n), 1)
    lane_row = lax.broadcasted_iota(jnp.int32, (1, n), 1)
    for start in range(0, n, block):
        spread = {j: jnp.broadcast_to(matrix[:, j:j + 1], (n, n)) for j in range(start, start + block)}
        for k in range(start, start + block):
            col = spread[k]
            inv = 1.0 / col[k:k + 1, :]
            scaled = jnp.where(lane_row == k, inv, matrix[k:k + 1, :] * inv)
            rest = jnp.where(lane_id == k, 0.0, matrix)
            matrix = jnp.where(row_id == k, scaled, rest - col * scaled)
            for j in range(k + 1, start + block):
                pivot_row = spread[j][k:k + 1, :] * inv
                spread[j] = jnp.where(row_id == k, pivot_row, spread[j] - col * pivot_row)
    return matrix


def kernel(sizes, tensor_ref, fbt_ref, fc_ref, out_ref,
           tbuf, fbt_own, fc_own, fb_send, fb_all, gc_all, gb_all, weights, sums, send, recv,
           load_sem, own_sem, line_sem, plane_sem, near_sem, far_sem, fb_s, fb_r, gc_s, gc_r, gb_s, gb_r, m_s, m_r):
    n_ia, n_ja, n_ka = sizes
    n_plane = n_ja * n_ka
    ia, ja, ka = lax.axis_index("ia"), lax.axis_index("ja"), lax.axis_index("ka")
    place = ja * n_ka + ka
    half = n_ia // 2
    mine = ia // half
    rank, shard = fbt_own.shape
    block_k = tbuf.shape[1]
    rows = out_ref.shape[0]
    group_rows = rows * n_ka
    groups = LANES // rank
    depth = half * shard

    def up(index, by, size):
        return lax.rem(index + by, size)

    def in_line(z):
        return {"ia": z}

    def in_plane(p):
        return {"ja": p // n_ka, "ka": p % n_ka}

    own_b = pltpu.make_async_copy(fbt_ref, fbt_own, own_sem.at[0])
    own_c = pltpu.make_async_copy(fc_ref, fc_own, own_sem.at[1])
    own_b.start()
    own_c.start()

    barrier = pltpu.get_barrier_semaphore()

    @pl.loop(ia + 1, n_ia)
    def _(z):
        pl.semaphore_signal(barrier, inc=1, device_id=in_line(z), device_id_type=MESH)

    @pl.when(ia == 0)
    def _():
        @pl.loop(place + 1, n_plane)
        def _(p):
            pl.semaphore_signal(barrier, inc=1, device_id=in_plane(p), device_id_type=MESH)

    def load(step):
        part = pl.ds(pl.multiple_of(step * group_rows, group_rows), group_rows)
        return pltpu.make_async_copy(tensor_ref.at[part], tbuf.at[part], load_sem.at[step])

    @pl.loop(0, n_ja)
    def _(step):
        load(step).start()

    own_b.wait()
    packed_rows = rank // 2
    own = fbt_own[...]
    packed_b = jnp.concatenate([own[:packed_rows], own[packed_rows:]], axis=1)
    fb_send[...] = packed_b
    fb_all[ia] = packed_b

    def push_rows(z):
        pltpu.make_async_remote_copy(
            fb_send, fb_all.at[ia], fb_s, fb_r.at[mine], device_id=in_line(z), device_id_type=MESH).start()

    def answer_rows(z):
        pl.semaphore_wait(line_sem.at[z], 1)
        push_rows(z)

    @pl.when(ia > 0)
    def _():
        pl.semaphore_wait(barrier, ia)

    @pl.when((ia == 0) & (place > 0))
    def _():
        pl.semaphore_wait(barrier, place)

    @pl.loop(0, ia)
    def _(z):
        push_rows(z)

    @pl.loop(0, ia)
    def _(z):
        pl.semaphore_signal(line_sem.at[ia], inc=1, device_id=in_line(z), device_id_type=MESH)

    @pl.when(ia == 0)
    def _():
        pl.semaphore_signal(plane_sem, inc=1)

        @pl.loop(0, place)
        def _(p):
            pl.semaphore_signal(plane_sem, inc=1, device_id=in_plane(p), device_id_type=MESH)

    pl.loop(ia + 1, (mine + 1) * half)(answer_rows)

    def await_rows(which, count):
        part = fb_all.at[pl.ds(0, count)]
        pltpu.make_async_copy(part, part, fb_r.at[which]).wait()

    def prepare(which):
        uppers, lowers = [], []
        for s in range(half):
            piece = fb_all[which * half + s]
            uppers.append(piece[:, :shard])
            lowers.append(piece[:, shard:])
        fbt = jnp.concatenate([jnp.concatenate(uppers, axis=1), jnp.concatenate(lowers, axis=1)], axis=0)
        high = fbt.astype(BF16)
        rest = fbt - high.astype(F32)
        middle = rest.astype(BF16)
        low = (rest - middle.astype(F32)).astype(BF16)
        stacked = jnp.concatenate([high.astype(F32), middle.astype(F32), low.astype(F32), jnp.zeros_like(fbt)], axis=0)
        weights[...] = stacked.T.astype(BF16)
        return fbt

    def gram_rows(fbt):
        gram = lax.dot_general(fbt, jnp.concatenate([fbt] * groups, axis=0), (((1,), (1,)), ((), ())),
                               precision=HIGHEST, preferred_element_type=F32)
        return pack_rows(gram, rank)

    def contract(step, which):
        columns = pl.ds(pl.multiple_of(which * depth, depth), depth)
        x = tbuf[pl.ds(pl.multiple_of(step * group_rows, group_rows), group_rows), :, columns].reshape(group_rows * block_k, depth)
        flat = jnp.dot(x, weights[...], preferred_element_type=F32).reshape(group_rows, block_k, LANES)
        return jnp.sum(flat * fc_tiled[None], axis=1)

    own_c.wait()
    fc_tiled = tile_lanes(fc_own[...])
    gc_all[0] = pack_rows(
        lax.dot_general(fc_own[...], fc_tiled, (((0,), (0,)), ((), ())), precision=HIGHEST, preferred_element_type=F32), rank)
    @pl.when(ia == 0)
    def _():
        pl.semaphore_wait(plane_sem, n_plane - place)

        @pl.loop(1, n_plane)
        def _(d):
            pl.semaphore_signal(near_sem, inc=1, device_id=in_plane(lax.rem(place + d, n_plane)), device_id_type=MESH)

    pl.loop(half + mine * half, n_ia)(answer_rows)

    @pl.when(ia == 0)
    def _():
        @pl.loop(1, n_ka)
        def _(d):
            pl.semaphore_signal(far_sem.at[0], inc=1, device_id={"ka": up(ka, d, n_ka)}, device_id_type=MESH)

    await_rows(mine, half - 1)
    gb_all[0] = gram_rows(prepare(mine))

    @pl.loop(0, n_ja)
    def _(step):
        load(step).wait()

    @pl.loop(0, n_ja, unroll=n_ja)
    def _(step):
        sums[step] = contract(step, mine)

    def tell(first, end):
        @pl.loop(first, end)
        def _(z):
            pl.semaphore_signal(plane_sem, inc=1, device_id=in_line(z), device_id_type=MESH)

    @pl.when(ia == 0)
    def _():
        pl.semaphore_wait(near_sem, n_plane - 1)
        tell(1, half)

    @pl.when(ia == 0)
    def _():
        pl.semaphore_wait(far_sem.at[0], n_ka - 1)

        @pl.loop(1, n_ja)
        def _(d):
            pl.semaphore_signal(far_sem.at[1], inc=1, device_id={"ja": up(ja, d, n_ja)}, device_id_type=MESH)

    await_rows(1 - mine, half)

    fbt = prepare(1 - mine)

    def push_grams():
        gb_all[0] = gb_all[0] + gram_rows(fbt)

        @pl.loop(1, n_ja)
        def _(d):
            pltpu.make_async_remote_copy(
                gb_all.at[0], gb_all.at[n_ja - d], gb_s, gb_r, device_id={"ja": up(ja, d, n_ja)}, device_id_type=MESH).start()

        @pl.loop(1, n_ka)
        def _(d):
            pltpu.make_async_remote_copy(
                gc_all.at[0], gc_all.at[n_ka - d], gc_s, gc_r, device_id={"ka": up(ka, d, n_ka)}, device_id_type=MESH).start()

    def finish(step):
        part = sums[step] + contract(step, 1 - mine)
        part = part + pltpu.roll(part, 2 * rank, 1)
        part = part + pltpu.roll(part, rank, 1)
        for b in range(n_ka):
            send[step * n_ka + b] = pack_rows(part[b * rows:(b + 1) * rows], rank)

    def push(to_j, to_k):
        pltpu.make_async_remote_copy(
            send.at[to_j * n_ka + to_k], recv.at[place], m_s, m_r, device_id={"ja": to_j, "ka": to_k}, device_id_type=MESH).start()

    def tell_upper():
        pl.semaphore_wait(far_sem.at[1], n_ja - 1)
        tell(half, n_ia)

    far_first = sorted(range(n_ja), key=lambda d: -min(d, n_ja - d))
    leading = [1, 0] + [d for d in far_first if d > 1]
    upper = (ia + n_ia - 1) // n_ia
    targets = [(1 - upper) * g + upper * up(ja, d, n_ja) for g, d in zip(leading, far_first)]
    far_k = sorted(range(1, n_ka), key=lambda d: -min(d, n_ka - d))
    done = 0
    for size in (1, 3, n_ja - 4):
        part = targets[done:done + size]
        for to_j in part:
            finish(to_j)
        if done == 0:
            pl.when(ia > 0)(functools.partial(pl.semaphore_wait, plane_sem, 1))
        for dk in far_k:
            for to_j in part:
                push(to_j, up(ka, dk, n_ka))
        for to_j in part:
            pl.when(to_j != ja)(functools.partial(push, to_j, ka))
        if done == 0:
            push_grams()
        done += size
        if done == 4:
            pl.when(ia == 0)(tell_upper)
    recv[place] = send[place]

    gc_part = gc_all.at[pl.ds(1, n_ka - 1)]
    gb_part = gb_all.at[pl.ds(1, n_ja - 1)]
    pltpu.make_async_copy(gc_part, gc_part, gc_r).wait()
    pltpu.make_async_copy(gb_part, gb_part, gb_r).wait()
    gram = jnp.sum(gc_all[...], axis=0) * jnp.sum(gb_all[...], axis=0)
    gram = jnp.concatenate([gram[:, g * rank:(g + 1) * rank] for g in range(groups)], axis=0)
    inverse = jnp.concatenate([inverse_spd(gram)] * groups, axis=0)

    fb_part = fb_all.at[pl.ds(0, n_ia - 1)]
    pltpu.make_async_copy(fb_part, fb_part, fb_s).wait()
    pltpu.make_async_copy(gc_part, gc_part, gc_s).wait()
    pltpu.make_async_copy(gb_part, gb_part, gb_s).wait()
    m_part = recv.at[pl.ds(0, n_plane - 1)]
    pltpu.make_async_copy(m_part, m_part, m_s).wait()
    pltpu.make_async_copy(m_part, m_part, m_r).wait()
    total = jnp.sum(recv[...], axis=0)
    lane = lane_group(total.shape, rank)
    spread = jnp.concatenate([jnp.where(lane == g, total, 0.0) for g in range(groups)], axis=0)
    out_ref[...] = jnp.dot(spread, inverse, precision=HIGHEST, preferred_element_type=F32)


def solution(mesh):
    sizes = (mesh.shape["ia"], mesh.shape["ja"], mesh.shape["ka"])
    n_ia, n_ja, n_ka = sizes

    def per_device(tensor, factor_b, factor_c):
        block_i, block_k, block_j = tensor.shape
        shard, rank = factor_b.shape
        rows = block_i // (n_ja * n_ka)
        groups = LANES // rank
        dma = pltpu.SemaphoreType.DMA
        vmem = pltpu.VMEM
        return pl.pallas_call(
            functools.partial(kernel, sizes),
            out_shape=pltpu.VMEM((rows, rank), F32),
            in_specs=[pl.BlockSpec(memory_space=pltpu.HBM)] * 3,
            out_specs=pl.BlockSpec(memory_space=pltpu.VMEM),
            scratch_shapes=[
                vmem((block_i, block_k, block_j), BF16),
                vmem((rank, shard), F32),
                vmem((block_k, rank), F32),
                vmem((rank // 2, 2 * shard), F32),
                vmem((n_ia, rank // 2, 2 * shard), F32),
                vmem((n_ka, rank // groups, LANES), F32),
                vmem((n_ja, rank // groups, LANES), F32),
                vmem((block_j // 2, LANES), BF16),
                vmem((n_ja, rows * n_ka, LANES), F32),
                vmem((n_ja * n_ka, rows // groups, LANES), F32),
                vmem((n_ja * n_ka, rows // groups, LANES), F32),
                dma((n_ja,)), dma((2,)),
                pltpu.SemaphoreType.REGULAR((n_ia,)), pltpu.SemaphoreType.REGULAR, pltpu.SemaphoreType.REGULAR, pltpu.SemaphoreType.REGULAR((2,)),
                dma, dma((2,)), dma, dma, dma, dma, dma, dma,
            ],
            compiler_params=pltpu.CompilerParams(collective_id=0, has_side_effects=True, vmem_limit_bytes=56 << 20),
        )(tensor, factor_b.T, factor_c)

    return jax.shard_map(
        per_device,
        mesh=mesh,
        in_specs=(P("ia", "ka", "ja"), P(("ja", "ia"), None), P("ka", None)),
        out_specs=P(("ia", "ja", "ka"), None),
        check_vma=False,
    )
```

```python
import functools

import jax
import jax.numpy as jnp
from jax import lax
from jax.experimental import pallas as pl
from jax.experimental.pallas import tpu as pltpu
from jax.sharding import PartitionSpec as P

MESH = pl.DeviceIdType.MESH
HIGHEST = lax.Precision.HIGHEST
F32 = jnp.float32
BF16 = jnp.bfloat16
LANES = 128


def lane_group(shape, rank):
    return lax.broadcasted_iota(jnp.int32, shape, 1) // rank


def tile_lanes(x):
    return jnp.concatenate([x] * (LANES // x.shape[1]), axis=1)


def pack_rows(x, rank):
    groups = LANES // rank
    m = x.shape[0] // groups
    lane = lane_group((m, LANES), rank)
    packed = x[:m]
    for g in range(1, groups):
        packed = jnp.where(lane == g, x[g * m:(g + 1) * m], packed)
    return packed


def inverse_spd(matrix, block=8):
    n = matrix.shape[0]
    row_id = lax.broadcasted_iota(jnp.int32, (n, n), 0)
    lane_id = lax.broadcasted_iota(jnp.int32, (n, n), 1)
    lane_row = lax.broadcasted_iota(jnp.int32, (1, n), 1)
    for start in range(0, n, block):
        spread = {j: jnp.broadcast_to(matrix[:, j:j + 1], (n, n)) for j in range(start, start + block)}
        for k in range(start, start + block):
            col = spread[k]
            inv = 1.0 / col[k:k + 1, :]
            scaled = jnp.where(lane_row == k, inv, matrix[k:k + 1, :] * inv)
            rest = jnp.where(lane_id == k, 0.0, matrix)
            matrix = jnp.where(row_id == k, scaled, rest - col * scaled)
            for j in range(k + 1, start + block):
                pivot_row = spread[j][k:k + 1, :] * inv
                spread[j] = jnp.where(row_id == k, pivot_row, spread[j] - col * pivot_row)
    return matrix


def kernel(sizes, tensor_ref, fbt_ref, fc_ref, out_ref,
           tbuf, fbt_own, fc_own, fb_send, fb_all, gc_all, gb_all, weights, sums, send, recv,
           load_sem, own_sem, line_sem, plane_sem, near_sem, far_sem, fb_s, fb_r, gc_s, gc_r, gb_s, gb_r, m_s, m_r):
    n_ia, n_ja, n_ka = sizes
    n_plane = n_ja * n_ka
    ia, ja, ka = lax.axis_index("ia"), lax.axis_index("ja"), lax.axis_index("ka")
    place = ja * n_ka + ka
    half = n_ia // 2
    mine = ia // half
    rank, shard = fbt_own.shape
    block_k = tbuf.shape[1]
    rows = out_ref.shape[0]
    group_rows = rows * n_ka
    groups = LANES // rank
    depth = half * shard

    def up(index, by, size):
        return lax.rem(index + by, size)

    def in_line(z):
        return {"ia": z}

    def in_plane(p):
        return {"ja": p // n_ka, "ka": p % n_ka}

    own_b = pltpu.make_async_copy(fbt_ref, fbt_own, own_sem.at[0])
    own_c = pltpu.make_async_copy(fc_ref, fc_own, own_sem.at[1])
    own_b.start()
    own_c.start()

    barrier = pltpu.get_barrier_semaphore()

    @pl.loop(ia + 1, n_ia)
    def _(z):
        pl.semaphore_signal(barrier, inc=1, device_id=in_line(z), device_id_type=MESH)

    @pl.when(ia == 0)
    def _():
        @pl.loop(place + 1, n_plane)
        def _(p):
            pl.semaphore_signal(barrier, inc=1, device_id=in_plane(p), device_id_type=MESH)

    def load(step):
        part = pl.ds(pl.multiple_of(step * group_rows, group_rows), group_rows)
        return pltpu.make_async_copy(tensor_ref.at[part], tbuf.at[part], load_sem.at[step])

    @pl.loop(0, n_ja)
    def _(step):
        load(step).start()

    own_b.wait()
    packed_rows = rank // 2
    own = fbt_own[...]
    packed_b = jnp.concatenate([own[:packed_rows], own[packed_rows:]], axis=1)
    fb_send[...] = packed_b
    fb_all[ia] = packed_b

    def push_rows(z):
        pltpu.make_async_remote_copy(
            fb_send, fb_all.at[ia], fb_s, fb_r.at[mine], device_id=in_line(z), device_id_type=MESH).start()

    def answer_rows(z):
        pl.semaphore_wait(line_sem.at[z], 1)
        push_rows(z)

    @pl.when(ia > 0)
    def _():
        pl.semaphore_wait(barrier, ia)

    @pl.when((ia == 0) & (place > 0))
    def _():
        pl.semaphore_wait(barrier, place)

    @pl.loop(0, ia)
    def _(z):
        push_rows(z)
        pl.semaphore_signal(line_sem.at[ia], inc=1, device_id=in_line(z), device_id_type=MESH)

    @pl.when(ia == 0)
    def _():
        pl.semaphore_signal(plane_sem, inc=1)

        @pl.loop(0, place)
        def _(p):
            pl.semaphore_signal(plane_sem, inc=1, device_id=in_plane(p), device_id_type=MESH)

    pl.loop(ia + 1, (mine + 1) * half)(answer_rows)

    def await_rows(which, count):
        part = fb_all.at[pl.ds(0, count)]
        pltpu.make_async_copy(part, part, fb_r.at[which]).wait()

    def prepare(which):
        uppers, lowers = [], []
        for s in range(half):
            piece = fb_all[which * half + s]
            uppers.append(piece[:, :shard])
            lowers.append(piece[:, shard:])
        fbt = jnp.concatenate([jnp.concatenate(uppers, axis=1), jnp.concatenate(lowers, axis=1)], axis=0)
        high = fbt.astype(BF16)
        rest = fbt - high.astype(F32)
        middle = rest.astype(BF16)
        low = (rest - middle.astype(F32)).astype(BF16)
        weights[...] = jnp.concatenate([high, middle, low, jnp.zeros_like(high)], axis=0)
        return fbt

    def gram_rows(fbt):
        gram = lax.dot_general(fbt, jnp.concatenate([fbt] * groups, axis=0), (((1,), (1,)), ((), ())),
                               precision=HIGHEST, preferred_element_type=F32)
        return pack_rows(gram, rank)

    def contract(step, which):
        columns = pl.ds(pl.multiple_of(which * depth, depth), depth)
        x = tbuf[pl.ds(pl.multiple_of(step * group_rows, group_rows), group_rows), :, columns].reshape(group_rows * block_k, depth)
        flat = lax.dot_general(x, weights[...], (((1,), (1,)), ((), ())), preferred_element_type=F32).reshape(group_rows, block_k, LANES)
        return jnp.sum(flat * fc_tiled[None], axis=1)

    own_c.wait()
    fc_tiled = tile_lanes(fc_own[...])
    gc_all[0] = pack_rows(
        lax.dot_general(fc_own[...], fc_tiled, (((0,), (0,)), ((), ())), precision=HIGHEST, preferred_element_type=F32), rank)
    @pl.when(ia == 0)
    def _():
        pl.semaphore_wait(plane_sem, n_plane - place)

        @pl.loop(1, n_plane)
        def _(d):
            pl.semaphore_signal(near_sem, inc=1, device_id=in_plane(lax.rem(place + d, n_plane)), device_id_type=MESH)

    pl.loop(half + mine * half, n_ia)(answer_rows)

    @pl.when(ia == 0)
    def _():
        @pl.loop(1, n_ka)
        def _(d):
            pl.semaphore_signal(far_sem.at[0], inc=1, device_id={"ka": up(ka, d, n_ka)}, device_id_type=MESH)

    await_rows(mine, half - 1)
    gb_all[0] = gram_rows(prepare(mine))

    @pl.loop(0, n_ja)
    def _(step):
        load(step).wait()

    @pl.loop(0, n_ja, unroll=n_ja)
    def _(step):
        sums[step] = contract(step, mine)

    def tell(first, end):
        @pl.loop(first, end)
        def _(z):
            pl.semaphore_signal(plane_sem, inc=1, device_id=in_line(z), device_id_type=MESH)

    @pl.when(ia == 0)
    def _():
        pl.semaphore_wait(near_sem, n_plane - 1)
        tell(1, half)

    @pl.when(ia == 0)
    def _():
        pl.semaphore_wait(far_sem.at[0], n_ka - 1)

        @pl.loop(1, n_ja)
        def _(d):
            pl.semaphore_signal(far_sem.at[1], inc=1, device_id={"ja": up(ja, d, n_ja)}, device_id_type=MESH)

    await_rows(1 - mine, half)

    fbt = prepare(1 - mine)

    def push_grams():
        gb_all[0] = gb_all[0] + gram_rows(fbt)

        @pl.loop(1, n_ja)
        def _(d):
            pltpu.make_async_remote_copy(
                gb_all.at[0], gb_all.at[n_ja - d], gb_s, gb_r, device_id={"ja": up(ja, d, n_ja)}, device_id_type=MESH).start()

        @pl.loop(1, n_ka)
        def _(d):
            pltpu.make_async_remote_copy(
                gc_all.at[0], gc_all.at[n_ka - d], gc_s, gc_r, device_id={"ka": up(ka, d, n_ka)}, device_id_type=MESH).start()

    def finish(step):
        part = sums[step] + contract(step, 1 - mine)
        part = part + pltpu.roll(part, 2 * rank, 1)
        part = part + pltpu.roll(part, rank, 1)
        for b in range(n_ka):
            send[step * n_ka + b] = pack_rows(part[b * rows:(b + 1) * rows], rank)

    def push(to_j, to_k):
        pltpu.make_async_remote_copy(
            send.at[to_j * n_ka + to_k], recv.at[place], m_s, m_r, device_id={"ja": to_j, "ka": to_k}, device_id_type=MESH).start()

    def tell_upper():
        pl.semaphore_wait(far_sem.at[1], n_ja - 1)
        tell(half, n_ia)

    targets = sorted(range(n_ja), key=lambda g: (g // 2, 1 - g % 2))
    targets = targets[:1] + targets[2:4] + targets[1:2] + targets[4:]
    far_k = sorted(range(1, n_ka), key=lambda d: -min(d, n_ka - d))
    done = 0
    for size in (1, 3, n_ja - 4):
        part = targets[done:done + size]
        for to_j in part:
            finish(to_j)
        if done == 0:
            pl.when(ia > 0)(functools.partial(pl.semaphore_wait, plane_sem, 1))
        for dk in far_k:
            for to_j in part:
                push(to_j, up(ka, dk, n_ka))
        for to_j in part:
            pl.when(to_j != ja)(functools.partial(push, to_j, ka))
        if done == 0:
            push_grams()
        done += size
        if done == 4:
            pl.when(ia == 0)(tell_upper)
    recv[place] = send[place]

    gc_part = gc_all.at[pl.ds(1, n_ka - 1)]
    gb_part = gb_all.at[pl.ds(1, n_ja - 1)]
    pltpu.make_async_copy(gc_part, gc_part, gc_r).wait()
    pltpu.make_async_copy(gb_part, gb_part, gb_r).wait()
    gram = jnp.sum(gc_all[...], axis=0) * jnp.sum(gb_all[...], axis=0)
    gram = jnp.concatenate([gram[:, g * rank:(g + 1) * rank] for g in range(groups)], axis=0)
    inverse = jnp.concatenate([inverse_spd(gram)] * groups, axis=0)

    fb_part = fb_all.at[pl.ds(0, n_ia - 1)]
    pltpu.make_async_copy(fb_part, fb_part, fb_s).wait()
    pltpu.make_async_copy(gc_part, gc_part, gc_s).wait()
    pltpu.make_async_copy(gb_part, gb_part, gb_s).wait()
    m_part = recv.at[pl.ds(0, n_plane - 1)]
    pltpu.make_async_copy(m_part, m_part, m_s).wait()
    pltpu.make_async_copy(m_part, m_part, m_r).wait()
    total = jnp.sum(recv[...], axis=0)
    lane = lane_group(total.shape, rank)
    spread = jnp.concatenate([jnp.where(lane == g, total, 0.0) for g in range(groups)], axis=0)
    out_ref[...] = jnp.dot(spread, inverse, precision=HIGHEST, preferred_element_type=F32)


def solution(mesh):
    sizes = (mesh.shape["ia"], mesh.shape["ja"], mesh.shape["ka"])
    n_ia, n_ja, n_ka = sizes

    def per_device(tensor, factor_b, factor_c):
        block_i, block_k, block_j = tensor.shape
        shard, rank = factor_b.shape
        rows = block_i // (n_ja * n_ka)
        groups = LANES // rank
        dma = pltpu.SemaphoreType.DMA
        vmem = pltpu.VMEM
        return pl.pallas_call(
            functools.partial(kernel, sizes),
            out_shape=pltpu.VMEM((rows, rank), F32),
            in_specs=[pl.BlockSpec(memory_space=pltpu.HBM)] * 3,
            out_specs=pl.BlockSpec(memory_space=pltpu.VMEM),
            scratch_shapes=[
                vmem((block_i, block_k, block_j), BF16),
                vmem((rank, shard), F32),
                vmem((block_k, rank), F32),
                vmem((rank // 2, 2 * shard), F32),
                vmem((n_ia, rank // 2, 2 * shard), F32),
                vmem((n_ka, rank // groups, LANES), F32),
                vmem((n_ja, rank // groups, LANES), F32),
                vmem((LANES, block_j // 2), BF16),
                vmem((n_ja, rows * n_ka, LANES), F32),
                vmem((n_ja * n_ka, rows // groups, LANES), F32),
                vmem((n_ja * n_ka, rows // groups, LANES), F32),
                dma((n_ja,)), dma((2,)),
                pltpu.SemaphoreType.REGULAR((n_ia,)), pltpu.SemaphoreType.REGULAR, pltpu.SemaphoreType.REGULAR, pltpu.SemaphoreType.REGULAR((2,)),
                dma, dma((2,)), dma, dma, dma, dma, dma, dma,
            ],
            compiler_params=pltpu.CompilerParams(collective_id=0, has_side_effects=True, vmem_limit_bytes=56 << 20),
        )(tensor, factor_b.T, factor_c)

    return jax.shard_map(
        per_device,
        mesh=mesh,
        in_specs=(P("ia", "ka", "ja"), P(("ja", "ia"), None), P("ka", None)),
        out_specs=P(("ia", "ja", "ka"), None),
        check_vma=False,
    )
```

```python
import functools

import jax
import jax.numpy as jnp
from jax import lax
from jax.experimental import pallas as pl
from jax.experimental.pallas import tpu as pltpu
from jax.sharding import PartitionSpec as P

MESH = pl.DeviceIdType.MESH
HIGHEST = lax.Precision.HIGHEST
F32 = jnp.float32
BF16 = jnp.bfloat16
LANES = 128


def lane_group(shape, rank):
    return lax.broadcasted_iota(jnp.int32, shape, 1) // rank


def tile_lanes(x):
    return jnp.concatenate([x] * (LANES // x.shape[1]), axis=1)


def pack_rows(x, rank):
    groups = LANES // rank
    m = x.shape[0] // groups
    lane = lane_group((m, LANES), rank)
    packed = x[:m]
    for g in range(1, groups):
        packed = jnp.where(lane == g, x[g * m:(g + 1) * m], packed)
    return packed


def inverse_spd(matrix, block=8):
    n = matrix.shape[0]
    row_id = lax.broadcasted_iota(jnp.int32, (n, n), 0)
    lane_id = lax.broadcasted_iota(jnp.int32, (n, n), 1)
    lane_row = lax.broadcasted_iota(jnp.int32, (1, n), 1)
    for start in range(0, n, block):
        spread = {j: jnp.broadcast_to(matrix[:, j:j + 1], (n, n)) for j in range(start, start + block)}
        for k in range(start, start + block):
            col = spread[k]
            inv = 1.0 / col[k:k + 1, :]
            scaled = jnp.where(lane_row == k, inv, matrix[k:k + 1, :] * inv)
            rest = jnp.where(lane_id == k, 0.0, matrix)
            matrix = jnp.where(row_id == k, scaled, rest - col * scaled)
            for j in range(k + 1, start + block):
                pivot_row = spread[j][k:k + 1, :] * inv
                spread[j] = jnp.where(row_id == k, pivot_row, spread[j] - col * pivot_row)
    return matrix


def kernel(sizes, tensor_ref, fbt_ref, fc_ref, out_ref,
           tbuf, fbt_own, fc_own, fb_send, fb_all, gc_all, gb_all, weights, sums, send, recv,
           load_sem, own_sem, line_sem, plane_sem, near_sem, far_sem, fb_s, fb_r, gc_s, gc_r, gb_s, gb_r, m_s, m_r):
    n_ia, n_ja, n_ka = sizes
    n_plane = n_ja * n_ka
    ia, ja, ka = lax.axis_index("ia"), lax.axis_index("ja"), lax.axis_index("ka")
    place = ja * n_ka + ka
    half = n_ia // 2
    mine = ia // half
    rank, shard = fbt_own.shape
    block_k = tbuf.shape[1]
    rows = out_ref.shape[0]
    group_rows = rows * n_ka
    groups = LANES // rank
    depth = half * shard

    def up(index, by, size):
        return lax.rem(index + by, size)

    def in_line(z):
        return {"ia": z}

    def in_plane(p):
        return {"ja": p // n_ka, "ka": p % n_ka}

    own_b = pltpu.make_async_copy(fbt_ref, fbt_own, own_sem.at[0])
    own_c = pltpu.make_async_copy(fc_ref, fc_own, own_sem.at[1])
    own_b.start()
    own_c.start()

    barrier = pltpu.get_barrier_semaphore()

    @pl.loop(ia + 1, n_ia)
    def _(z):
        pl.semaphore_signal(barrier, inc=1, device_id=in_line(z), device_id_type=MESH)

    @pl.when(ia == 0)
    def _():
        @pl.loop(place + 1, n_plane)
        def _(p):
            pl.semaphore_signal(barrier, inc=1, device_id=in_plane(p), device_id_type=MESH)

    def load(step):
        part = pl.ds(pl.multiple_of(step * group_rows, group_rows), group_rows)
        return pltpu.make_async_copy(tensor_ref.at[part], tbuf.at[part], load_sem.at[step])

    @pl.loop(0, n_ja)
    def _(step):
        load(step).start()

    own_b.wait()
    packed_rows = rank // 2
    own = fbt_own[...]
    packed_b = jnp.concatenate([own[:packed_rows], own[packed_rows:]], axis=1)
    fb_send[...] = packed_b
    fb_all[ia] = packed_b

    def push_rows(z):
        pltpu.make_async_remote_copy(
            fb_send, fb_all.at[ia], fb_s, fb_r.at[mine], device_id=in_line(z), device_id_type=MESH).start()

    def answer_rows(z):
        pl.semaphore_wait(line_sem.at[z], 1)
        push_rows(z)

    @pl.when(ia > 0)
    def _():
        pl.semaphore_wait(barrier, ia)

    @pl.when((ia == 0) & (place > 0))
    def _():
        pl.semaphore_wait(barrier, place)

    @pl.loop(0, ia)
    def _(z):
        push_rows(z)
        pl.semaphore_signal(line_sem.at[ia], inc=1, device_id=in_line(z), device_id_type=MESH)

    @pl.when(ia == 0)
    def _():
        pl.semaphore_signal(plane_sem, inc=1)

        @pl.loop(0, place)
        def _(p):
            pl.semaphore_signal(plane_sem, inc=1, device_id=in_plane(p), device_id_type=MESH)

    pl.loop(ia + 1, (mine + 1) * half)(answer_rows)

    def await_rows(which, count):
        part = fb_all.at[pl.ds(0, count)]
        pltpu.make_async_copy(part, part, fb_r.at[which]).wait()

    def prepare(which):
        uppers, lowers = [], []
        for s in range(half):
            piece = fb_all[which * half + s]
            uppers.append(piece[:, :shard])
            lowers.append(piece[:, shard:])
        fbt = jnp.concatenate([jnp.concatenate(uppers, axis=1), jnp.concatenate(lowers, axis=1)], axis=0)
        high = fbt.astype(BF16)
        rest = fbt - high.astype(F32)
        middle = rest.astype(BF16)
        low = (rest - middle.astype(F32)).astype(BF16)
        weights[...] = jnp.concatenate([high, middle, low, jnp.zeros_like(high)], axis=0)
        return fbt

    def gram_rows(fbt):
        gram = lax.dot_general(fbt, jnp.concatenate([fbt] * groups, axis=0), (((1,), (1,)), ((), ())),
                               precision=HIGHEST, preferred_element_type=F32)
        return pack_rows(gram, rank)

    def contract(step, which):
        columns = pl.ds(pl.multiple_of(which * depth, depth), depth)
        x = tbuf[pl.ds(pl.multiple_of(step * group_rows, group_rows), group_rows), :, columns].reshape(group_rows * block_k, depth)
        flat = lax.dot_general(x, weights[...], (((1,), (1,)), ((), ())), preferred_element_type=F32).reshape(group_rows, block_k, LANES)
        return jnp.sum(flat * fc_tiled[None], axis=1)

    own_c.wait()
    fc_tiled = tile_lanes(fc_own[...])
    gc_all[0] = pack_rows(
        lax.dot_general(fc_own[...], fc_tiled, (((0,), (0,)), ((), ())), precision=HIGHEST, preferred_element_type=F32), rank)
    @pl.when(ia == 0)
    def _():
        pl.semaphore_wait(plane_sem, n_plane - place)

        @pl.loop(1, n_plane)
        def _(d):
            pl.semaphore_signal(near_sem, inc=1, device_id=in_plane(lax.rem(place + d, n_plane)), device_id_type=MESH)

    pl.loop(half + mine * half, n_ia)(answer_rows)

    @pl.when(ia == 0)
    def _():
        @pl.loop(1, n_ka)
        def _(d):
            pl.semaphore_signal(far_sem.at[0], inc=1, device_id={"ka": up(ka, d, n_ka)}, device_id_type=MESH)

    await_rows(mine, half - 1)
    gb_all[0] = gram_rows(prepare(mine))

    @pl.loop(0, n_ja)
    def _(step):
        load(step).wait()

    @pl.loop(0, n_ja, unroll=n_ja)
    def _(step):
        sums[step] = contract(step, mine)

    def tell(first, end):
        @pl.loop(first, end)
        def _(z):
            pl.semaphore_signal(plane_sem, inc=1, device_id=in_line(z), device_id_type=MESH)

    @pl.when(ia == 0)
    def _():
        pl.semaphore_wait(near_sem, n_plane - 1)
        tell(1, half)

    @pl.when(ia == 0)
    def _():
        pl.semaphore_wait(far_sem.at[0], n_ka - 1)

        @pl.loop(1, n_ja)
        def _(d):
            pl.semaphore_signal(far_sem.at[1], inc=1, device_id={"ja": up(ja, d, n_ja)}, device_id_type=MESH)

    await_rows(1 - mine, half)

    fbt = prepare(1 - mine)

    def push_grams():
        gb_all[0] = gb_all[0] + gram_rows(fbt)

        @pl.loop(1, n_ja)
        def _(d):
            pltpu.make_async_remote_copy(
                gb_all.at[0], gb_all.at[n_ja - d], gb_s, gb_r, device_id={"ja": up(ja, d, n_ja)}, device_id_type=MESH).start()

        @pl.loop(1, n_ka)
        def _(d):
            pltpu.make_async_remote_copy(
                gc_all.at[0], gc_all.at[n_ka - d], gc_s, gc_r, device_id={"ka": up(ka, d, n_ka)}, device_id_type=MESH).start()

    def finish(step):
        part = sums[step] + contract(step, 1 - mine)
        part = part + pltpu.roll(part, 2 * rank, 1)
        part = part + pltpu.roll(part, rank, 1)
        for b in range(n_ka):
            send[step * n_ka + b] = pack_rows(part[b * rows:(b + 1) * rows], rank)

    def push(to_j, to_k):
        pltpu.make_async_remote_copy(
            send.at[to_j * n_ka + to_k], recv.at[place], m_s, m_r, device_id={"ja": to_j, "ka": to_k}, device_id_type=MESH).start()

    def tell_upper():
        pl.semaphore_wait(far_sem.at[1], n_ja - 1)
        tell(half, n_ia)

    targets = sorted(range(n_ja), key=lambda g: (g // 2, 1 - g % 2))
    targets = targets[:1] + targets[2:4] + targets[1:2] + targets[4:]
    far_k = sorted(range(1, n_ka), key=lambda d: -min(d, n_ka - d))
    first, second, third = targets[:1], targets[1:n_ja // 2], targets[n_ja // 2:]

    def push_rows_of(part):
        for dk in far_k:
            for to_j in part:
                push(to_j, up(ka, dk, n_ka))
        for to_j in part:
            pl.when(to_j != ja)(functools.partial(push, to_j, ka))

    def open_plane():
        pl.when(ia > 0)(functools.partial(pl.semaphore_wait, plane_sem, 1))
        push_rows_of(first)
        push_grams()

    for to_j in first:
        finish(to_j)
    pl.when(mine == 0)(open_plane)
    for to_j in second:
        finish(to_j)
    pl.when(mine == 1)(open_plane)
    push_rows_of(second)
    pl.when(ia == 0)(tell_upper)
    for to_j in third:
        finish(to_j)
    push_rows_of(third)
    recv[place] = send[place]

    gc_part = gc_all.at[pl.ds(1, n_ka - 1)]
    gb_part = gb_all.at[pl.ds(1, n_ja - 1)]
    pltpu.make_async_copy(gc_part, gc_part, gc_r).wait()
    pltpu.make_async_copy(gb_part, gb_part, gb_r).wait()
    gram = jnp.sum(gc_all[...], axis=0) * jnp.sum(gb_all[...], axis=0)
    gram = jnp.concatenate([gram[:, g * rank:(g + 1) * rank] for g in range(groups)], axis=0)
    inverse = jnp.concatenate([inverse_spd(gram)] * groups, axis=0)

    fb_part = fb_all.at[pl.ds(0, n_ia - 1)]
    pltpu.make_async_copy(fb_part, fb_part, fb_s).wait()
    pltpu.make_async_copy(gc_part, gc_part, gc_s).wait()
    pltpu.make_async_copy(gb_part, gb_part, gb_s).wait()
    m_part = recv.at[pl.ds(0, n_plane - 1)]
    pltpu.make_async_copy(m_part, m_part, m_s).wait()
    pltpu.make_async_copy(m_part, m_part, m_r).wait()
    total = jnp.sum(recv[...], axis=0)
    lane = lane_group(total.shape, rank)
    spread = jnp.concatenate([jnp.where(lane == g, total, 0.0) for g in range(groups)], axis=0)
    out_ref[...] = jnp.dot(spread, inverse, precision=HIGHEST, preferred_element_type=F32)


def solution(mesh):
    sizes = (mesh.shape["ia"], mesh.shape["ja"], mesh.shape["ka"])
    n_ia, n_ja, n_ka = sizes

    def per_device(tensor, factor_b, factor_c):
        block_i, block_k, block_j = tensor.shape
        shard, rank = factor_b.shape
        rows = block_i // (n_ja * n_ka)
        groups = LANES // rank
        dma = pltpu.SemaphoreType.DMA
        vmem = pltpu.VMEM
        return pl.pallas_call(
            functools.partial(kernel, sizes),
            out_shape=pltpu.VMEM((rows, rank), F32),
            in_specs=[pl.BlockSpec(memory_space=pltpu.HBM)] * 3,
            out_specs=pl.BlockSpec(memory_space=pltpu.VMEM),
            scratch_shapes=[
                vmem((block_i, block_k, block_j), BF16),
                vmem((rank, shard), F32),
                vmem((block_k, rank), F32),
                vmem((rank // 2, 2 * shard), F32),
                vmem((n_ia, rank // 2, 2 * shard), F32),
                vmem((n_ka, rank // groups, LANES), F32),
                vmem((n_ja, rank // groups, LANES), F32),
                vmem((LANES, block_j // 2), BF16),
                vmem((n_ja, rows * n_ka, LANES), F32),
                vmem((n_ja * n_ka, rows // groups, LANES), F32),
                vmem((n_ja * n_ka, rows // groups, LANES), F32),
                dma((n_ja,)), dma((2,)),
                pltpu.SemaphoreType.REGULAR((n_ia,)), pltpu.SemaphoreType.REGULAR, pltpu.SemaphoreType.REGULAR, pltpu.SemaphoreType.REGULAR((2,)),
                dma, dma((2,)), dma, dma, dma, dma, dma, dma,
            ],
            compiler_params=pltpu.CompilerParams(collective_id=0, has_side_effects=True, vmem_limit_bytes=56 << 20),
        )(tensor, factor_b.T, factor_c)

    return jax.shard_map(
        per_device,
        mesh=mesh,
        in_specs=(P("ia", "ka", "ja"), P(("ja", "ia"), None), P("ka", None)),
        out_specs=P(("ia", "ja", "ka"), None),
        check_vma=False,
    )
```

```python
import functools

import jax
import jax.numpy as jnp
from jax import lax
from jax.experimental import pallas as pl
from jax.experimental.pallas import tpu as pltpu
from jax.sharding import PartitionSpec as P

MESH = pl.DeviceIdType.MESH
HIGHEST = lax.Precision.HIGHEST
F32 = jnp.float32
BF16 = jnp.bfloat16
LANES = 128


def lane_group(shape, rank):
    return lax.broadcasted_iota(jnp.int32, shape, 1) // rank


def tile_lanes(x):
    return jnp.concatenate([x] * (LANES // x.shape[1]), axis=1)


def pack_rows(x, rank):
    groups = LANES // rank
    m = x.shape[0] // groups
    lane = lane_group((m, LANES), rank)
    packed = x[:m]
    for g in range(1, groups):
        packed = jnp.where(lane == g, x[g * m:(g + 1) * m], packed)
    return packed


def inverse_spd(matrix, block=8):
    n = matrix.shape[0]
    row_id = lax.broadcasted_iota(jnp.int32, (n, n), 0)
    lane_id = lax.broadcasted_iota(jnp.int32, (n, n), 1)
    lane_row = lax.broadcasted_iota(jnp.int32, (1, n), 1)
    for start in range(0, n, block):
        spread = {j: jnp.broadcast_to(matrix[:, j:j + 1], (n, n)) for j in range(start, start + block)}
        for k in range(start, start + block):
            col = spread[k]
            inv = 1.0 / col[k:k + 1, :]
            scaled = jnp.where(lane_row == k, inv, matrix[k:k + 1, :] * inv)
            rest = jnp.where(lane_id == k, 0.0, matrix)
            matrix = jnp.where(row_id == k, scaled, rest - col * scaled)
            for j in range(k + 1, start + block):
                pivot_row = spread[j][k:k + 1, :] * inv
                spread[j] = jnp.where(row_id == k, pivot_row, spread[j] - col * pivot_row)
    return matrix


def kernel(sizes, tensor_ref, fbt_ref, fc_ref, out_ref,
           tbuf, fbt_own, fc_own, fb_send, fb_all, gc_all, gb_all, weights, sums, send, recv,
           load_sem, own_sem, line_sem, plane_sem, near_sem, far_sem, fb_s, fb_r, gc_s, gc_r, gb_s, gb_r, m_s, m_r):
    n_ia, n_ja, n_ka = sizes
    n_plane = n_ja * n_ka
    ia, ja, ka = lax.axis_index("ia"), lax.axis_index("ja"), lax.axis_index("ka")
    place = ja * n_ka + ka
    half = n_ia // 2
    mine = ia // half
    rank, shard = fbt_own.shape
    block_k = tbuf.shape[1]
    rows = out_ref.shape[0]
    group_rows = rows * n_ka
    groups = LANES // rank
    depth = half * shard

    def up(index, by, size):
        return lax.rem(index + by, size)

    def in_line(z):
        return {"ia": z}

    def in_plane(p):
        return {"ja": p // n_ka, "ka": p % n_ka}

    own_b = pltpu.make_async_copy(fbt_ref, fbt_own, own_sem.at[0])
    own_c = pltpu.make_async_copy(fc_ref, fc_own, own_sem.at[1])
    own_b.start()
    own_c.start()

    barrier = pltpu.get_barrier_semaphore()

    @pl.loop(ia + 1, n_ia)
    def _(z):
        pl.semaphore_signal(barrier, inc=1, device_id=in_line(z), device_id_type=MESH)

    @pl.when(ia == 0)
    def _():
        @pl.loop(place + 1, n_plane)
        def _(p):
            pl.semaphore_signal(barrier, inc=1, device_id=in_plane(p), device_id_type=MESH)

    def load(step):
        part = pl.ds(pl.multiple_of(step * group_rows, group_rows), group_rows)
        return pltpu.make_async_copy(tensor_ref.at[part], tbuf.at[part], load_sem.at[step])

    own_b.wait()
    packed_rows = rank // 2
    own = fbt_own[...]
    packed_b = jnp.concatenate([own[:packed_rows], own[packed_rows:]], axis=1)
    fb_send[...] = packed_b
    fb_all[ia] = packed_b

    def push_rows(z):
        pltpu.make_async_remote_copy(
            fb_send, fb_all.at[ia], fb_s, fb_r.at[mine], device_id=in_line(z), device_id_type=MESH).start()

    def answer_rows(z):
        pl.semaphore_wait(line_sem.at[z], 1)
        push_rows(z)

    @pl.when(ia > 0)
    def _():
        pl.semaphore_wait(barrier, ia)

    @pl.when((ia == 0) & (place > 0))
    def _():
        pl.semaphore_wait(barrier, place)

    @pl.loop(0, ia)
    def _(z):
        push_rows(z)
        pl.semaphore_signal(line_sem.at[ia], inc=1, device_id=in_line(z), device_id_type=MESH)

    @pl.when(ia == 0)
    def _():
        pl.semaphore_signal(plane_sem, inc=1)

        @pl.loop(0, place)
        def _(p):
            pl.semaphore_signal(plane_sem, inc=1, device_id=in_plane(p), device_id_type=MESH)

    @pl.loop(0, n_ja)
    def _(step):
        load(step).start()

    pl.loop(ia + 1, (mine + 1) * half)(answer_rows)

    def await_rows(which, count):
        part = fb_all.at[pl.ds(0, count)]
        pltpu.make_async_copy(part, part, fb_r.at[which]).wait()

    def prepare(which):
        uppers, lowers = [], []
        for s in range(half):
            piece = fb_all[which * half + s]
            uppers.append(piece[:, :shard])
            lowers.append(piece[:, shard:])
        fbt = jnp.concatenate([jnp.concatenate(uppers, axis=1), jnp.concatenate(lowers, axis=1)], axis=0)
        high = fbt.astype(BF16)
        rest = fbt - high.astype(F32)
        middle = rest.astype(BF16)
        low = (rest - middle.astype(F32)).astype(BF16)
        weights[...] = jnp.concatenate([high, middle, low, jnp.zeros_like(high)], axis=0)
        return fbt

    def gram_rows(fbt):
        gram = lax.dot_general(fbt, jnp.concatenate([fbt] * groups, axis=0), (((1,), (1,)), ((), ())),
                               precision=HIGHEST, preferred_element_type=F32)
        return pack_rows(gram, rank)

    def contract(step, which):
        columns = pl.ds(pl.multiple_of(which * depth, depth), depth)
        x = tbuf[pl.ds(pl.multiple_of(step * group_rows, group_rows), group_rows), :, columns].reshape(group_rows * block_k, depth)
        flat = lax.dot_general(x, weights[...], (((1,), (1,)), ((), ())), preferred_element_type=F32).reshape(group_rows, block_k, LANES)
        return jnp.sum(flat * fc_tiled[None], axis=1)

    own_c.wait()
    fc_tiled = tile_lanes(fc_own[...])
    gc_all[0] = pack_rows(
        lax.dot_general(fc_own[...], fc_tiled, (((0,), (0,)), ((), ())), precision=HIGHEST, preferred_element_type=F32), rank)
    @pl.when(ia == 0)
    def _():
        pl.semaphore_wait(plane_sem, n_plane - place)

        @pl.loop(1, n_plane)
        def _(d):
            pl.semaphore_signal(near_sem, inc=1, device_id=in_plane(lax.rem(place + d, n_plane)), device_id_type=MESH)

    pl.loop(half + mine * half, n_ia)(answer_rows)

    @pl.when(ia == 0)
    def _():
        @pl.loop(1, n_ka)
        def _(d):
            pl.semaphore_signal(far_sem.at[0], inc=1, device_id={"ka": up(ka, d, n_ka)}, device_id_type=MESH)

    await_rows(mine, half - 1)
    gb_all[0] = gram_rows(prepare(mine))

    @pl.loop(0, n_ja)
    def _(step):
        load(step).wait()

    @pl.loop(0, n_ja, unroll=n_ja)
    def _(step):
        sums[step] = contract(step, mine)

    def tell(first, end):
        @pl.loop(first, end)
        def _(z):
            pl.semaphore_signal(plane_sem, inc=1, device_id=in_line(z), device_id_type=MESH)

    @pl.when(ia == 0)
    def _():
        pl.semaphore_wait(near_sem, n_plane - 1)
        tell(1, half)

    @pl.when(ia == 0)
    def _():
        pl.semaphore_wait(far_sem.at[0], n_ka - 1)

        @pl.loop(1, n_ja)
        def _(d):
            pl.semaphore_signal(far_sem.at[1], inc=1, device_id={"ja": up(ja, d, n_ja)}, device_id_type=MESH)

    await_rows(1 - mine, half)

    fbt = prepare(1 - mine)

    def push_grams():
        gb_all[0] = gb_all[0] + gram_rows(fbt)

        @pl.loop(1, n_ja)
        def _(d):
            pltpu.make_async_remote_copy(
                gb_all.at[0], gb_all.at[n_ja - d], gb_s, gb_r, device_id={"ja": up(ja, d, n_ja)}, device_id_type=MESH).start()

        @pl.loop(1, n_ka)
        def _(d):
            pltpu.make_async_remote_copy(
                gc_all.at[0], gc_all.at[n_ka - d], gc_s, gc_r, device_id={"ka": up(ka, d, n_ka)}, device_id_type=MESH).start()

    def finish(step):
        part = sums[step] + contract(step, 1 - mine)
        part = part + pltpu.roll(part, 2 * rank, 1)
        part = part + pltpu.roll(part, rank, 1)
        for b in range(n_ka):
            send[step * n_ka + b] = pack_rows(part[b * rows:(b + 1) * rows], rank)

    def push(to_j, to_k):
        pltpu.make_async_remote_copy(
            send.at[to_j * n_ka + to_k], recv.at[place], m_s, m_r, device_id={"ja": to_j, "ka": to_k}, device_id_type=MESH).start()

    def tell_upper():
        pl.semaphore_wait(far_sem.at[1], n_ja - 1)
        tell(half, n_ia)

    targets = sorted(range(n_ja), key=lambda g: (g // 2, 1 - g % 2))
    targets = targets[:1] + targets[2:4] + targets[1:2] + targets[4:]
    far_k = sorted(range(1, n_ka), key=lambda d: -min(d, n_ka - d))
    first, second, third = targets[:1], targets[1:n_ja // 2], targets[n_ja // 2:]

    def push_rows_of(part):
        for dk in far_k:
            for to_j in part:
                push(to_j, up(ka, dk, n_ka))
        for to_j in part:
            pl.when(to_j != ja)(functools.partial(push, to_j, ka))

    def open_plane():
        pl.when(ia > 0)(functools.partial(pl.semaphore_wait, plane_sem, 1))
        push_rows_of(first)
        push_grams()

    for to_j in first:
        finish(to_j)
    pl.when(mine == 0)(open_plane)
    for to_j in second:
        finish(to_j)
    pl.when(mine == 1)(open_plane)
    push_rows_of(second)
    pl.when(ia == 0)(tell_upper)
    for to_j in third:
        finish(to_j)
    push_rows_of(third)
    recv[place] = send[place]

    gc_part = gc_all.at[pl.ds(1, n_ka - 1)]
    gb_part = gb_all.at[pl.ds(1, n_ja - 1)]
    pltpu.make_async_copy(gc_part, gc_part, gc_r).wait()
    pltpu.make_async_copy(gb_part, gb_part, gb_r).wait()
    gram = jnp.sum(gc_all[...], axis=0) * jnp.sum(gb_all[...], axis=0)
    gram = jnp.concatenate([gram[:, g * rank:(g + 1) * rank] for g in range(groups)], axis=0)
    inverse = jnp.concatenate([inverse_spd(gram)] * groups, axis=0)

    fb_part = fb_all.at[pl.ds(0, n_ia - 1)]
    pltpu.make_async_copy(fb_part, fb_part, fb_s).wait()
    pltpu.make_async_copy(gc_part, gc_part, gc_s).wait()
    pltpu.make_async_copy(gb_part, gb_part, gb_s).wait()
    m_part = recv.at[pl.ds(0, n_plane - 1)]
    pltpu.make_async_copy(m_part, m_part, m_s).wait()
    pltpu.make_async_copy(m_part, m_part, m_r).wait()
    total = jnp.sum(recv[...], axis=0)
    lane = lane_group(total.shape, rank)
    spread = jnp.concatenate([jnp.where(lane == g, total, 0.0) for g in range(groups)], axis=0)
    out_ref[...] = jnp.dot(spread, inverse, precision=HIGHEST, preferred_element_type=F32)


def solution(mesh):
    sizes = (mesh.shape["ia"], mesh.shape["ja"], mesh.shape["ka"])
    n_ia, n_ja, n_ka = sizes

    def per_device(tensor, factor_b, factor_c):
        block_i, block_k, block_j = tensor.shape
        shard, rank = factor_b.shape
        rows = block_i // (n_ja * n_ka)
        groups = LANES // rank
        dma = pltpu.SemaphoreType.DMA
        vmem = pltpu.VMEM
        return pl.pallas_call(
            functools.partial(kernel, sizes),
            out_shape=pltpu.VMEM((rows, rank), F32),
            in_specs=[pl.BlockSpec(memory_space=pltpu.HBM)] * 3,
            out_specs=pl.BlockSpec(memory_space=pltpu.VMEM),
            scratch_shapes=[
                vmem((block_i, block_k, block_j), BF16),
                vmem((rank, shard), F32),
                vmem((block_k, rank), F32),
                vmem((rank // 2, 2 * shard), F32),
                vmem((n_ia, rank // 2, 2 * shard), F32),
                vmem((n_ka, rank // groups, LANES), F32),
                vmem((n_ja, rank // groups, LANES), F32),
                vmem((LANES, block_j // 2), BF16),
                vmem((n_ja, rows * n_ka, LANES), F32),
                vmem((n_ja * n_ka, rows // groups, LANES), F32),
                vmem((n_ja * n_ka, rows // groups, LANES), F32),
                dma((n_ja,)), dma((2,)),
                pltpu.SemaphoreType.REGULAR((n_ia,)), pltpu.SemaphoreType.REGULAR, pltpu.SemaphoreType.REGULAR, pltpu.SemaphoreType.REGULAR((2,)),
                dma, dma((2,)), dma, dma, dma, dma, dma, dma,
            ],
            compiler_params=pltpu.CompilerParams(collective_id=0, has_side_effects=True, vmem_limit_bytes=56 << 20),
        )(tensor, factor_b.T, factor_c)

    return jax.shard_map(
        per_device,
        mesh=mesh,
        in_specs=(P("ia", "ka", "ja"), P(("ja", "ia"), None), P("ka", None)),
        out_specs=P(("ia", "ja", "ka"), None),
        check_vma=False,
    )
```

```python
import functools

import jax
import jax.numpy as jnp
from jax import lax
from jax.experimental import pallas as pl
from jax.experimental.pallas import tpu as pltpu
from jax.sharding import PartitionSpec as P

MESH = pl.DeviceIdType.MESH
HIGHEST = lax.Precision.HIGHEST
F32 = jnp.float32
BF16 = jnp.bfloat16
LANES = 128


def lane_group(shape, rank):
    return lax.broadcasted_iota(jnp.int32, shape, 1) // rank


def tile_lanes(x):
    return jnp.concatenate([x] * (LANES // x.shape[1]), axis=1)


def pack_rows(x, rank):
    groups = LANES // rank
    m = x.shape[0] // groups
    lane = lane_group((m, LANES), rank)
    packed = x[:m]
    for g in range(1, groups):
        packed = jnp.where(lane == g, x[g * m:(g + 1) * m], packed)
    return packed


def inverse_spd(matrix, block=8):
    n = matrix.shape[0]
    row_id = lax.broadcasted_iota(jnp.int32, (n, n), 0)
    lane_id = lax.broadcasted_iota(jnp.int32, (n, n), 1)
    lane_row = lax.broadcasted_iota(jnp.int32, (1, n), 1)
    for start in range(0, n, block):
        spread = {j: jnp.broadcast_to(matrix[:, j:j + 1], (n, n)) for j in range(start, start + block)}
        for k in range(start, start + block):
            col = spread[k]
            inv = 1.0 / col[k:k + 1, :]
            scaled = jnp.where(lane_row == k, inv, matrix[k:k + 1, :] * inv)
            rest = jnp.where(lane_id == k, 0.0, matrix)
            matrix = jnp.where(row_id == k, scaled, rest - col * scaled)
            for j in range(k + 1, start + block):
                pivot_row = spread[j][k:k + 1, :] * inv
                spread[j] = jnp.where(row_id == k, pivot_row, spread[j] - col * pivot_row)
    return matrix


def kernel(sizes, tensor_ref, fbt_ref, fc_ref, out_ref,
           tbuf, fbt_own, fc_own, fb_send, fb_all, gc_all, gb_all, weights, sums, send, recv,
           load_sem, own_sem, line_sem, plane_sem, near_sem, far_sem, fb_s, fb_r, gc_s, gc_r, gb_s, gb_r, m_s, m_r):
    n_ia, n_ja, n_ka = sizes
    n_plane = n_ja * n_ka
    ia, ja, ka = lax.axis_index("ia"), lax.axis_index("ja"), lax.axis_index("ka")
    place = ja * n_ka + ka
    half = n_ia // 2
    mine = ia // half
    rank, shard = fbt_own.shape
    block_k = tbuf.shape[1]
    rows = out_ref.shape[0]
    group_rows = rows * n_ka
    groups = LANES // rank
    depth = half * shard

    def up(index, by, size):
        return lax.rem(index + by, size)

    def in_line(z):
        return {"ia": z}

    def in_plane(p):
        return {"ja": p // n_ka, "ka": p % n_ka}

    own_b = pltpu.make_async_copy(fbt_ref, fbt_own, own_sem.at[0])
    own_c = pltpu.make_async_copy(fc_ref, fc_own, own_sem.at[1])
    own_b.start()
    own_c.start()

    barrier = pltpu.get_barrier_semaphore()

    @pl.loop(ia + 1, n_ia)
    def _(z):
        pl.semaphore_signal(barrier, inc=1, device_id=in_line(z), device_id_type=MESH)

    @pl.when(ia == 0)
    def _():
        @pl.loop(place + 1, n_plane)
        def _(p):
            pl.semaphore_signal(barrier, inc=1, device_id=in_plane(p), device_id_type=MESH)

    def load(step):
        part = pl.ds(pl.multiple_of(step * group_rows, group_rows), group_rows)
        return pltpu.make_async_copy(tensor_ref.at[part], tbuf.at[part], load_sem.at[step])

    own_b.wait()
    packed_rows = rank // 2
    own = fbt_own[...]
    packed_b = jnp.concatenate([own[:packed_rows], own[packed_rows:]], axis=1)
    fb_send[...] = packed_b
    fb_all[ia] = packed_b

    def push_rows(z):
        pltpu.make_async_remote_copy(
            fb_send, fb_all.at[ia], fb_s, fb_r.at[mine], device_id=in_line(z), device_id_type=MESH).start()

    def answer_rows(z):
        pl.semaphore_wait(line_sem.at[z], 1)
        push_rows(z)

    @pl.when(ia > 0)
    def _():
        pl.semaphore_wait(barrier, ia)

    @pl.when((ia == 0) & (place > 0))
    def _():
        pl.semaphore_wait(barrier, place)

    @pl.loop(0, ia)
    def _(z):
        push_rows(z)
        pl.semaphore_signal(line_sem.at[ia], inc=1, device_id=in_line(z), device_id_type=MESH)

    @pl.when(ia == 0)
    def _():
        pl.semaphore_signal(plane_sem, inc=1)

        @pl.loop(0, place)
        def _(p):
            pl.semaphore_signal(plane_sem, inc=1, device_id=in_plane(p), device_id_type=MESH)

    @pl.loop(0, n_ja)
    def _(step):
        load(step).start()

    pl.loop(ia + 1, (mine + 1) * half)(answer_rows)

    def await_rows(which, count):
        part = fb_all.at[pl.ds(0, count)]
        pltpu.make_async_copy(part, part, fb_r.at[which]).wait()

    def prepare(which):
        uppers, lowers = [], []
        for s in range(half):
            piece = fb_all[which * half + s]
            uppers.append(piece[:, :shard])
            lowers.append(piece[:, shard:])
        fbt = jnp.concatenate([jnp.concatenate(uppers, axis=1), jnp.concatenate(lowers, axis=1)], axis=0)
        high = fbt.astype(BF16)
        rest = fbt - high.astype(F32)
        middle = rest.astype(BF16)
        low = (rest - middle.astype(F32)).astype(BF16)
        weights[...] = jnp.concatenate([high, middle, low, jnp.zeros_like(high)], axis=0)
        return fbt

    def gram_rows(fbt):
        gram = lax.dot_general(fbt, jnp.concatenate([fbt] * groups, axis=0), (((1,), (1,)), ((), ())),
                               precision=HIGHEST, preferred_element_type=F32)
        return pack_rows(gram, rank)

    def contract(step, which, low=0, high=n_ka):
        columns = pl.ds(pl.multiple_of(which * depth, depth), depth)
        count = (high - low) * rows
        x = tbuf[pl.ds(pl.multiple_of(step * group_rows + low * rows, rows), count), :, columns].reshape(count * block_k, depth)
        flat = lax.dot_general(x, weights[...], (((1,), (1,)), ((), ())), preferred_element_type=F32).reshape(count, block_k, LANES)
        return jnp.sum(flat * fc_tiled[None], axis=1)

    own_c.wait()
    fc_tiled = tile_lanes(fc_own[...])
    gc_all[0] = pack_rows(
        lax.dot_general(fc_own[...], fc_tiled, (((0,), (0,)), ((), ())), precision=HIGHEST, preferred_element_type=F32), rank)
    @pl.when(ia == 0)
    def _():
        pl.semaphore_wait(plane_sem, n_plane - place)

        @pl.loop(1, n_plane)
        def _(d):
            pl.semaphore_signal(near_sem, inc=1, device_id=in_plane(lax.rem(place + d, n_plane)), device_id_type=MESH)

    pl.loop(half + mine * half, n_ia)(answer_rows)

    @pl.when(ia == 0)
    def _():
        @pl.loop(1, n_ka)
        def _(d):
            pl.semaphore_signal(far_sem.at[0], inc=1, device_id={"ka": up(ka, d, n_ka)}, device_id_type=MESH)

    await_rows(mine, half - 1)
    gb_all[0] = gram_rows(prepare(mine))

    @pl.loop(0, n_ja)
    def _(step):
        load(step).wait()

    @pl.loop(0, n_ja, unroll=n_ja)
    def _(step):
        sums[step] = contract(step, mine)

    def tell(first, end):
        @pl.loop(first, end)
        def _(z):
            pl.semaphore_signal(plane_sem, inc=1, device_id=in_line(z), device_id_type=MESH)

    @pl.when(ia == 0)
    def _():
        pl.semaphore_wait(near_sem, n_plane - 1)
        tell(1, half)

    @pl.when(ia == 0)
    def _():
        pl.semaphore_wait(far_sem.at[0], n_ka - 1)

        @pl.loop(1, n_ja)
        def _(d):
            pl.semaphore_signal(far_sem.at[1], inc=1, device_id={"ja": up(ja, d, n_ja)}, device_id_type=MESH)

    await_rows(1 - mine, half)

    fbt = prepare(1 - mine)

    def push_grams():
        gb_all[0] = gb_all[0] + gram_rows(fbt)

        @pl.loop(1, n_ja)
        def _(d):
            pltpu.make_async_remote_copy(
                gb_all.at[0], gb_all.at[n_ja - d], gb_s, gb_r, device_id={"ja": up(ja, d, n_ja)}, device_id_type=MESH).start()

        @pl.loop(1, n_ka)
        def _(d):
            pltpu.make_async_remote_copy(
                gc_all.at[0], gc_all.at[n_ka - d], gc_s, gc_r, device_id={"ka": up(ka, d, n_ka)}, device_id_type=MESH).start()

    def finish(step, low=0, high=n_ka):
        part = sums[step, low * rows:high * rows] + contract(step, 1 - mine, low, high)
        part = part + pltpu.roll(part, 2 * rank, 1)
        part = part + pltpu.roll(part, rank, 1)
        for b in range(low, high):
            send[step * n_ka + b] = pack_rows(part[(b - low) * rows:(b - low + 1) * rows], rank)

    def push(to_j, to_k):
        pltpu.make_async_remote_copy(
            send.at[to_j * n_ka + to_k], recv.at[place], m_s, m_r, device_id={"ja": to_j, "ka": to_k}, device_id_type=MESH).start()

    def tell_upper():
        pl.semaphore_wait(far_sem.at[1], n_ja - 1)
        tell(half, n_ia)

    targets = sorted(range(n_ja), key=lambda g: (g // 2, 1 - g % 2))
    targets = targets[:1] + targets[2:4] + targets[1:2] + targets[4:]
    far_k = sorted(range(1, n_ka), key=lambda d: -min(d, n_ka - d))
    head, second, third = targets[0], targets[1:n_ja // 2], targets[n_ja // 2:]

    def push_rows_of(part):
        for dk in far_k:
            for to_j in part:
                push(to_j, up(ka, dk, n_ka))
        for to_j in part:
            pl.when(to_j != ja)(functools.partial(push, to_j, ka))

    def push_head(low, high):
        for k in range(low, high):
            pl.when(place != head * n_ka + k)(functools.partial(push, head, k))

    def open_plane():
        pl.when(ia > 0)(functools.partial(pl.semaphore_wait, plane_sem, 1))
        push_head(0, 1)

    def push_rest():
        push_head(1, n_ka)
        push_grams()

    finish(head, 0, 1)
    pl.when(mine == 0)(open_plane)
    finish(head, 1, n_ka)
    pl.when(mine == 0)(push_rest)
    for to_j in second:
        finish(to_j)
    pl.when(mine == 1)(open_plane)
    pl.when(mine == 1)(push_rest)
    push_rows_of(second)
    pl.when(ia == 0)(tell_upper)
    for to_j in third:
        finish(to_j)
    push_rows_of(third)
    recv[place] = send[place]

    gc_part = gc_all.at[pl.ds(1, n_ka - 1)]
    gb_part = gb_all.at[pl.ds(1, n_ja - 1)]
    pltpu.make_async_copy(gc_part, gc_part, gc_r).wait()
    pltpu.make_async_copy(gb_part, gb_part, gb_r).wait()
    gram = jnp.sum(gc_all[...], axis=0) * jnp.sum(gb_all[...], axis=0)
    gram = jnp.concatenate([gram[:, g * rank:(g + 1) * rank] for g in range(groups)], axis=0)
    inverse = jnp.concatenate([inverse_spd(gram)] * groups, axis=0)

    fb_part = fb_all.at[pl.ds(0, n_ia - 1)]
    pltpu.make_async_copy(fb_part, fb_part, fb_s).wait()
    pltpu.make_async_copy(gc_part, gc_part, gc_s).wait()
    pltpu.make_async_copy(gb_part, gb_part, gb_s).wait()
    m_part = recv.at[pl.ds(0, n_plane - 1)]
    pltpu.make_async_copy(m_part, m_part, m_s).wait()
    pltpu.make_async_copy(m_part, m_part, m_r).wait()
    total = jnp.sum(recv[...], axis=0)
    lane = lane_group(total.shape, rank)
    spread = jnp.concatenate([jnp.where(lane == g, total, 0.0) for g in range(groups)], axis=0)
    out_ref[...] = jnp.dot(spread, inverse, precision=HIGHEST, preferred_element_type=F32)


def solution(mesh):
    sizes = (mesh.shape["ia"], mesh.shape["ja"], mesh.shape["ka"])
    n_ia, n_ja, n_ka = sizes

    def per_device(tensor, factor_b, factor_c):
        block_i, block_k, block_j = tensor.shape
        shard, rank = factor_b.shape
        rows = block_i // (n_ja * n_ka)
        groups = LANES // rank
        dma = pltpu.SemaphoreType.DMA
        vmem = pltpu.VMEM
        return pl.pallas_call(
            functools.partial(kernel, sizes),
            out_shape=pltpu.VMEM((rows, rank), F32),
            in_specs=[pl.BlockSpec(memory_space=pltpu.HBM)] * 3,
            out_specs=pl.BlockSpec(memory_space=pltpu.VMEM),
            scratch_shapes=[
                vmem((block_i, block_k, block_j), BF16),
                vmem((rank, shard), F32),
                vmem((block_k, rank), F32),
                vmem((rank // 2, 2 * shard), F32),
                vmem((n_ia, rank // 2, 2 * shard), F32),
                vmem((n_ka, rank // groups, LANES), F32),
                vmem((n_ja, rank // groups, LANES), F32),
                vmem((LANES, block_j // 2), BF16),
                vmem((n_ja, rows * n_ka, LANES), F32),
                vmem((n_ja * n_ka, rows // groups, LANES), F32),
                vmem((n_ja * n_ka, rows // groups, LANES), F32),
                dma((n_ja,)), dma((2,)),
                pltpu.SemaphoreType.REGULAR((n_ia,)), pltpu.SemaphoreType.REGULAR, pltpu.SemaphoreType.REGULAR, pltpu.SemaphoreType.REGULAR((2,)),
                dma, dma((2,)), dma, dma, dma, dma, dma, dma,
            ],
            compiler_params=pltpu.CompilerParams(collective_id=0, has_side_effects=True, vmem_limit_bytes=56 << 20),
        )(tensor, factor_b.T, factor_c)

    return jax.shard_map(
        per_device,
        mesh=mesh,
        in_specs=(P("ia", "ka", "ja"), P(("ja", "ia"), None), P("ka", None)),
        out_specs=P(("ia", "ja", "ka"), None),
        check_vma=False,
    )
```
